32 devices in a mesh: seq: 16 (over z, x, core), head: 2 (over y).
Axes of the slice: x: 2, y: 2, z: 4, core: 2. Of those that a mesh axis runs over, the one named last changes fastest.
Arguments:
- queries: bfloat16 [8192, 8192], P(('seq', 'head')), may hold values from -9 to 9
- keys: bfloat16 [8192, 1024], P(('seq', 'head')), may hold values from -9 to 9
- values: bfloat16 [8192, 1024], P(('seq', 'head')), may hold values from -6 to 6
- prefix_keys: bfloat16 [32768, 1024], P('seq', 'head'), may hold values from -6 to 6
- prefix_values: bfloat16 [32768, 1024], P('seq', 'head'), may hold values from -6 to 6
- roles: int32 [64], P('head'), may hold values from 0 to 1, as said below
- columns: int32 [64, 6], P('head'), may hold values from 0 to 479, as said below
- col_count: int32 [64], P('head'), may hold values from 1 to 6, as said below
- diagonals: int32 [64, 4], P('head'), may hold values from 0 to 7, as said below
Outputs:
- attended: bfloat16 [8192, 8192], P('seq', 'head')
The draws below stay inside these ranges and needn't reach their ends.
Inputs may be any that keep to these rules, and one draw needn't show every extreme that they name: `roles`: 1 marks a retrieval head, 0 a passing head; at most 4 retrieval heads share one key-value head, and some key-value head has exactly 4. `columns`: prefix block indices, blocks of 64 cache rows, distinct within a head. `col_count`: some retrieval head uses all 6 of its column blocks. `diagonals`: distinct within a head; the first offset of every head is 0.
All inputs are finite; a program needn't handle non-finite values.
Results may differ from the reference program's by a relative error of at most 0.0049.
Values may be sent and summed in bfloat16 or wider, within the bound.
A program may use at most 128 MiB of HBM per device.

```python
import math
import jax
import jax.numpy as jnp
from jax import lax

QUERY_HEADS = 64
KEY_VALUE_HEADS = 8
HEAD_SIZE = 128
P_DEV = 2048
SINK = 128
WIN = 512
BLK = 64
VB = 6
NSL = 4
MAX_RETRIEVERS = 4
SPAN_TOKENS = 8192
PREFIX_TOKENS = 32768


def draw_queries(key, part):
    drawn_random = jax.random.fold_in(key, 3)
    final_output = jnp.clip(2.0 * jax.random.normal(drawn_random, (SPAN_TOKENS, QUERY_HEADS * HEAD_SIZE), jnp.float32), -8.0, 8.0)
    return final_output.astype(jnp.bfloat16)


def draw_keys(key, part):
    drawn_random = jax.random.fold_in(key, 5)
    final_output = jnp.clip(jax.random.normal(drawn_random, (SPAN_TOKENS, KEY_VALUE_HEADS * HEAD_SIZE), jnp.float32), -4.0, 4.0)
    return final_output.astype(jnp.bfloat16)


def role_table(key):
    count_random, pinned_random, score_random = jax.random.split(jax.random.fold_in(key, 21), 3)
    group_share = QUERY_HEADS // KEY_VALUE_HEADS
    count_list = jax.random.randint(count_random, (KEY_VALUE_HEADS,), 0, MAX_RETRIEVERS + 1)
    pinned_choice = jax.random.randint(pinned_random, (), 0, KEY_VALUE_HEADS)
    count_list = jnp.where(jnp.arange(KEY_VALUE_HEADS) == pinned_choice, MAX_RETRIEVERS, count_list)
    score_matrix = jax.random.randint(score_random, (KEY_VALUE_HEADS, group_share), 0, 1 << 20) * group_share + jnp.arange(group_share)[None, :]
    ranking_lookup = jnp.argsort(jnp.argsort(score_matrix, axis=1), axis=1)
    chosen = ranking_lookup < count_list[:, None]
    front_entries = (ranking_lookup == 0) & (jnp.arange(KEY_VALUE_HEADS) == pinned_choice)[:, None]
    return (chosen.reshape(QUERY_HEADS).astype(jnp.int32), front_entries.reshape(QUERY_HEADS))


def draw_roles(key, part):
    chosen, front_entries = role_table(key)
    return chosen


def draw_col_count(key, part):
    chosen, front_entries = role_table(key)
    drawn = jax.random.randint(jax.random.fold_in(key, 23), (QUERY_HEADS,), 1, VB + 1)
    return jnp.where(front_entries, VB, drawn).astype(jnp.int32)


def draw_columns(key, part):
    allowed_blocks = (PREFIX_TOKENS - P_DEV) // BLK
    head_keys = jax.random.split(jax.random.fold_in(key, 31), QUERY_HEADS)

    def pick_blocks(head_key):
        return jax.random.permutation(head_key, allowed_blocks)[:VB]
    return jax.vmap(pick_blocks)(head_keys).astype(jnp.int32)


def draw_diagonals(key, part):
    head_keys = jax.random.split(jax.random.fold_in(key, 41), QUERY_HEADS)

    def pick_offsets(head_key):
        return jax.random.permutation(head_key, WIN // BLK - 1)[:NSL - 1] + 1
    others = jax.vmap(pick_offsets)(head_keys)
    return jnp.concatenate([jnp.zeros((QUERY_HEADS, 1), jnp.int32), others.astype(jnp.int32)], 1)


def block_scale(key, shape, cuts, low, largest):
    factor_of = 1.0
    for dim, blocks in cuts:
        heights = jax.random.uniform(jax.random.fold_in(jax.random.fold_in(key, 6), dim), (blocks,), jnp.float32, low / len(cuts), largest / len(cuts))
        factor_of = factor_of * jnp.repeat(jnp.exp(heights), shape[dim] // blocks).reshape((-1,) + (1,) * (len(shape) - 1 - dim))
    return factor_of


def gaussian(rng, shape, spread, limit, cuts=(), kind=jnp.bfloat16):
    values = jax.random.normal(rng, shape, jnp.float32) * spread
    if len(cuts) > 0:
        values = block_scale(rng, shape, cuts, -0.22, 0.18) * values
    return jnp.clip(values, min=-limit, max=limit).astype(kind)


def setup_inputs(seed: int = 0) -> dict:
    streams_of = jax.random.split(jax.random.key(seed), 10)
    return {
        "queries": draw_queries(jax.random.fold_in(streams_of[9], 71), 0),
        "keys": draw_keys(jax.random.fold_in(streams_of[9], 71), 0),
        "values": gaussian(streams_of[2], (SPAN_TOKENS, KEY_VALUE_HEADS * HEAD_SIZE), 1.0, 6.0, ((0, 32),)),
        "prefix_keys": gaussian(streams_of[3], (PREFIX_TOKENS, KEY_VALUE_HEADS * HEAD_SIZE), 1.0, 6.0, ((0, 16), (1, 2))),
        "prefix_values": gaussian(streams_of[4], (PREFIX_TOKENS, KEY_VALUE_HEADS * HEAD_SIZE), 1.0, 6.0, ((0, 16), (1, 2))),
        "roles": draw_roles(jax.random.fold_in(streams_of[9], 71), 0),
        "columns": draw_columns(jax.random.fold_in(streams_of[9], 71), 0),
        "col_count": draw_col_count(jax.random.fold_in(streams_of[9], 71), 0),
        "diagonals": draw_diagonals(jax.random.fold_in(streams_of[9], 71), 0),
    }


def masked_softmax(score_matrix, allowed):
    row_max = lax.optimization_barrier(jnp.max(jnp.where(allowed, score_matrix, -jnp.inf), axis=-1, keepdims=True))
    expo = jnp.where(allowed, jnp.exp(score_matrix - row_max), 0.0)
    total = lax.optimization_barrier(jnp.sum(expo, axis=-1, keepdims=True))
    return (expo / total).astype(jnp.bfloat16)

def passing(q_head, k_head, v_head):
    scaling = 1.0 / math.sqrt(HEAD_SIZE)
    offset_grid = jnp.arange(2 * WIN)[None, :] - jnp.arange(WIN)[:, None]
    band_ok = (offset_grid >= 1) & (offset_grid <= WIN)
    allowed = jnp.concatenate([jnp.ones((WIN, SINK), dtype=jnp.bool_), band_ok], 1)
    sink_k = k_head[:SINK]
    sink_v = v_head[:SINK]

    def one_block(which):
        q_rows = lax.dynamic_slice_in_dim(q_head, (which * WIN).astype(jnp.int32), WIN, 0)
        start = (PREFIX_TOKENS - WIN + which * WIN).astype(jnp.int32)
        band_k = lax.dynamic_slice_in_dim(k_head, start, 2 * WIN, 0)
        band_v = lax.dynamic_slice_in_dim(v_head, start, 2 * WIN, 0)
        keys_here = jnp.concatenate([sink_k, band_k], 0)
        vals_here = jnp.concatenate([sink_v, band_v], 0)
        score_matrix = jnp.dot(q_rows, keys_here.T, preferred_element_type=jnp.float32) * scaling
        probs = masked_softmax(score_matrix, allowed)
        return jnp.dot(probs, vals_here, preferred_element_type=jnp.float32)
    final_output = lax.map(one_block, jnp.arange(SPAN_TOKENS // WIN, dtype=jnp.int32))
    return final_output.reshape(SPAN_TOKENS, HEAD_SIZE)

def retrieval(q_head, k_head, v_head, cols, count_used, offsets_d):
    scaling = 1.0 / math.sqrt(HEAD_SIZE)
    vert_k = k_head[:PREFIX_TOKENS].reshape(PREFIX_TOKENS // BLK, BLK, HEAD_SIZE)[cols].reshape(VB * BLK, HEAD_SIZE)
    vert_v = v_head[:PREFIX_TOKENS].reshape(PREFIX_TOKENS // BLK, BLK, HEAD_SIZE)[cols].reshape(VB * BLK, HEAD_SIZE)
    key_blocks = k_head.reshape((PREFIX_TOKENS + SPAN_TOKENS) // BLK, BLK, HEAD_SIZE)
    val_blocks = v_head.reshape((PREFIX_TOKENS + SPAN_TOKENS) // BLK, BLK, HEAD_SIZE)
    per_rows = WIN // BLK
    vert_ok = jnp.arange(VB * BLK) // BLK < count_used
    within = jnp.arange(BLK)[None, :] <= jnp.arange(BLK)[:, None]
    slash_ok = (offsets_d[:, None, None] > 0) | within[None, :, :]
    slash_ok = jnp.transpose(slash_ok, (1, 0, 2)).reshape(BLK, NSL * BLK)
    allowed = jnp.concatenate([jnp.broadcast_to(vert_ok[None, :], (BLK, VB * BLK)), slash_ok], 1)

    def one_block(which):
        q_rows = lax.dynamic_slice_in_dim(q_head, (which * WIN).astype(jnp.int32), WIN, 0)
        picks = (PREFIX_TOKENS // BLK + which * per_rows + jnp.arange(per_rows))[:, None] - offsets_d[None, :]
        slash_k = key_blocks[picks].reshape(per_rows, NSL * BLK, HEAD_SIZE)
        slash_v = val_blocks[picks].reshape(per_rows, NSL * BLK, HEAD_SIZE)
        q_blocks = q_rows.reshape(per_rows, BLK, HEAD_SIZE)
        vert_scores = jnp.dot(q_rows, vert_k.T, preferred_element_type=jnp.float32) * scaling
        vert_scores = vert_scores.reshape(per_rows, BLK, VB * BLK)
        slash_scores = jnp.einsum('nqd,nkd->nqk', q_blocks.astype(jnp.float32), slash_k.astype(jnp.float32)) * scaling
        score_matrix = jnp.concatenate([vert_scores, slash_scores], -1)
        probs = masked_softmax(score_matrix, allowed[None, :, :])
        vert_part = jnp.dot(probs[:, :, :VB * BLK].reshape(WIN, VB * BLK), vert_v, preferred_element_type=jnp.float32)
        slash_part = jnp.einsum('nqk,nkd->nqd', probs[:, :, VB * BLK:].astype(jnp.float32), slash_v.astype(jnp.float32))
        return vert_part + slash_part.reshape(WIN, HEAD_SIZE)
    final_output = lax.map(one_block, jnp.arange(SPAN_TOKENS // WIN, dtype=jnp.int32))
    return final_output.reshape(SPAN_TOKENS, HEAD_SIZE)

def reference(queries, keys, values, prefix_keys, prefix_values, roles, columns, col_count, diagonals):
    all_keys = jnp.concatenate([prefix_keys, keys], 0)
    all_values = jnp.concatenate([prefix_values, values], 0)
    group_share = QUERY_HEADS // KEY_VALUE_HEADS

    def one_head(head_index):
        kv_head = head_index // group_share
        q_head = lax.dynamic_slice_in_dim(queries, (head_index * HEAD_SIZE).astype(jnp.int32), HEAD_SIZE, 1)
        k_head = lax.dynamic_slice_in_dim(all_keys, (kv_head * HEAD_SIZE).astype(jnp.int32), HEAD_SIZE, 1)
        v_head = lax.dynamic_slice_in_dim(all_values, (kv_head * HEAD_SIZE).astype(jnp.int32), HEAD_SIZE, 1)
        final_output = lax.cond(roles[head_index] == 1, lambda: retrieval(q_head, k_head, v_head, columns[head_index], col_count[head_index], diagonals[head_index]), lambda: passing(q_head, k_head, v_head))
        return final_output.astype(jnp.bfloat16)
    per_head = lax.map(one_head, jnp.arange(QUERY_HEADS, dtype=jnp.int32))
    return jnp.transpose(per_head, (1, 0, 2)).reshape(SPAN_TOKENS, QUERY_HEADS * HEAD_SIZE)
```

```python
import functools
import math

import jax
import jax.numpy as jnp
from jax import lax
from jax.experimental import pallas as pl
from jax.experimental.pallas import tpu as pltpu
from jax.sharding import PartitionSpec as P

QUERY_HEADS = 64
KEY_VALUE_HEADS = 8
SHARE = QUERY_HEADS // KEY_VALUE_HEADS
D = 128
SINK = 128
WIN = 512
BLK = 64
VB = 6
NSL = 4
MAX_RETRIEVERS = 4
QB = 128
SCALE = math.log2(math.e) / math.sqrt(D)
VMEM_LIMIT = 40 * 1024 * 1024


def dot_nt(a, b):
    return lax.dot_general(a, b, (((1,), (1,)), ((), ())), preferred_element_type=jnp.float32)


def dot(a, b):
    return jnp.dot(a, b, preferred_element_type=jnp.float32)


def collect_kernel(own, blk, kv_of, pk, pv, out, sem):
    count = own.shape[0]
    out[...] = jnp.zeros_like(out)

    def copies(t):
        rows = pl.ds(pl.multiple_of(blk[t] * BLK, BLK), BLK)
        cols = pl.ds(pl.multiple_of(kv_of[t] * D, D), D)
        place = pl.ds(pl.multiple_of(t * BLK, BLK), BLK)
        return (
            pltpu.make_async_copy(pk.at[rows, cols], out.at[place, pl.ds(0, D)], sem.at[0, t]),
            pltpu.make_async_copy(pv.at[rows, cols], out.at[place, pl.ds(D, D)], sem.at[1, t]),
        )

    def start(t, carry):
        @pl.when(own[t] == 1)
        def _():
            for copy in copies(t):
                copy.start()

        return carry

    def finish(t, carry):
        @pl.when(own[t] == 1)
        def _():
            for copy in copies(t):
                copy.wait()

        return carry

    lax.fori_loop(0, count, start, 0)
    lax.fori_loop(0, count, finish, 0)


def collect(own, blk, kv_of, prefix_keys, prefix_values):
    count = own.shape[0]
    return pl.pallas_call(
        collect_kernel,
        grid_spec=pltpu.PrefetchScalarGridSpec(
            num_scalar_prefetch=3,
            grid=(1,),
            in_specs=[pl.BlockSpec(memory_space=pl.ANY)] * 2,
            out_specs=pl.BlockSpec((count * BLK, 2 * D), lambda i, *_: (0, 0)),
            scratch_shapes=[pltpu.SemaphoreType.DMA((2, count))],
        ),
        out_shape=jax.ShapeDtypeStruct((count * BLK, 2 * D), jnp.bfloat16),
        compiler_params=pltpu.CompilerParams(vmem_limit_bytes=VMEM_LIMIT),
        name="collect_columns",
    )(own, blk, kv_of, prefix_keys, prefix_values)


def new_group(heads, i):
    before = heads[jnp.maximum(i - 1, 0)]
    return (i == 0) | (heads[i] // SHARE != before // SHARE)


def passing_kernel(heads, used, q, k, v, pk, pv, sk, sv, out, keys_t, vals):
    i = pl.program_id(0)
    rows = q.shape[0]

    @pl.when(new_group(heads, i))
    def _():
        keys_t[:, :SINK] = sk[...].T
        keys_t[:, SINK : SINK + WIN] = pk[...].T
        keys_t[:, SINK + WIN :] = k[...].T
        vals[:SINK, :D] = sv[...]
        vals[SINK : SINK + WIN, :D] = pv[...]
        vals[SINK + WIN :, :D] = v[...]
        vals[:, D:] = jnp.ones_like(vals[:, D:])

    @pl.when(i < used[0])
    def _():
        row = lax.broadcasted_iota(jnp.int32, (QB, QB), 0)
        col = lax.broadcasted_iota(jnp.int32, (QB, QB), 1)
        for r in range(0, rows, QB):
            low, high = SINK + r, SINK + r + WIN + QB
            window = jnp.concatenate([keys_t[:, :SINK], keys_t[:, low:high]], 1)
            s = dot(q[r : r + QB, :], window)
            s = jnp.concatenate(
                [
                    s[:, :SINK],
                    jnp.where(col > row, s[:, SINK : SINK + QB], -jnp.inf),
                    s[:, SINK + QB : SINK + WIN],
                    jnp.where(col <= row, s[:, SINK + WIN :], -jnp.inf),
                ],
                1,
            )
            top = jnp.max(s, axis=1, keepdims=True)
            p = jnp.exp2((s - top) * SCALE).astype(jnp.bfloat16)
            acc = dot(p, jnp.concatenate([vals[:SINK, :], vals[low:high, :]], 0))
            out[r : r + QB, :] = (acc[:, :D] / acc[:, D:]).astype(out.dtype)


def passing(heads, used, q, kv, previous, sink):
    rows, width = q.shape
    kv_count = kv.shape[1] // (2 * D)

    def head(i, heads, used):
        return (0, heads[i])

    def key(i, heads, used):
        return (0, heads[i] // SHARE)

    def value(i, heads, used):
        return (0, kv_count + heads[i] // SHARE)

    return pl.pallas_call(
        passing_kernel,
        grid_spec=pltpu.PrefetchScalarGridSpec(
            num_scalar_prefetch=2,
            grid=(heads.shape[0],),
            in_specs=[
                pl.BlockSpec((rows, D), head),
                pl.BlockSpec((rows, D), key),
                pl.BlockSpec((rows, D), value),
                pl.BlockSpec((WIN, D), key),
                pl.BlockSpec((WIN, D), value),
                pl.BlockSpec((SINK, D), key),
                pl.BlockSpec((SINK, D), value),
            ],
            out_specs=pl.BlockSpec((rows, D), head),
            scratch_shapes=[
                pltpu.VMEM((D, SINK + WIN + rows), jnp.bfloat16),
                pltpu.VMEM((SINK + WIN + rows, 2 * D), jnp.bfloat16),
            ],
        ),
        out_shape=jax.ShapeDtypeStruct((rows, width), jnp.bfloat16),
        compiler_params=pltpu.CompilerParams(vmem_limit_bytes=VMEM_LIMIT),
        cost_estimate=pl.CostEstimate(
            flops=4 * width * rows * (SINK + WIN + QB) * 2,
            bytes_accessed=4 * rows * width,
            transcendentals=width // D * rows * (SINK + WIN + QB),
        ),
        name="passing_heads",
    )(heads, used, q, kv, kv, previous, previous, sink, sink)


def retrieval_kernel(
    heads, used, counts, offsets, q, k, v, pk, pv, vert, old, out, keys, vals, sem
):
    i = pl.program_id(0)
    rows = q.shape[0]

    @pl.when(new_group(heads, i))
    def _():
        keys[:WIN, :] = pk[...]
        keys[WIN:, :] = k[...]
        vals[:WIN, :D] = pv[...]
        vals[WIN:, :D] = v[...]
        vals[:, D:] = jnp.ones_like(vals[:, D:])

    @pl.when((i == 0) & (used[0] == 0))
    def _():
        copy = pltpu.make_async_copy(old.at[:, pl.ds(0, D)], out, sem)
        copy.start()
        copy.wait()

    @pl.when(i < used[0])
    def _():
        row = lax.broadcasted_iota(jnp.int32, (BLK, NSL * BLK), 0)
        col = lax.broadcasted_iota(jnp.int32, (BLK, NSL * BLK), 1)
        causal = (col <= row) | (col >= BLK)
        lane = lax.broadcasted_iota(jnp.int32, (1, VB * BLK), 1)
        open_cols = lane < counts[i] * BLK
        vert_k = vert[:, :D]
        vert_v = jnp.concatenate([vert[:, D:], jnp.ones((VB * BLK, D), jnp.bfloat16)], 1)
        for r in range(0, rows, QB):
            q_rows = q[r : r + QB, :]
            s_vert = jnp.where(open_cols, dot_nt(q_rows, vert_k), -jnp.inf)
            p_verts, slashes = [], []
            for b in range(0, QB, BLK):
                picks = [
                    pl.ds(
                        pl.multiple_of((WIN + r + b) - offsets[i * NSL + t] * BLK, BLK), BLK
                    )
                    for t in range(NSL)
                ]
                near_k = jnp.concatenate([keys[pick, :] for pick in picks], 0)
                near_v = jnp.concatenate([vals[pick, :] for pick in picks], 0)
                s_near = jnp.where(causal, dot_nt(q_rows[b : b + BLK], near_k), -jnp.inf)
                s_far = s_vert[b : b + BLK]
                top = jnp.maximum(
                    jnp.max(s_near, axis=1, keepdims=True), jnp.max(s_far, axis=1, keepdims=True)
                )
                p_near = jnp.exp2((s_near - top) * SCALE).astype(jnp.bfloat16)
                p_verts.append(jnp.exp2((s_far - top) * SCALE).astype(jnp.bfloat16))
                slashes.append(dot(p_near, near_v))
            acc = dot(jnp.concatenate(p_verts, 0), vert_v) + jnp.concatenate(slashes, 0)
            out[r : r + QB, :] = (acc[:, :D] / acc[:, D:]).astype(out.dtype)


def retrieval(heads, used, counts, offsets, q, kv, previous, vertical, old):
    rows, width = q.shape
    kv_count = kv.shape[1] // (2 * D)
    slots = heads.shape[0]

    def head(i, heads, *_):
        return (0, heads[i])

    def key(i, heads, *_):
        return (0, heads[i] // SHARE)

    def value(i, heads, *_):
        return (0, kv_count + heads[i] // SHARE)

    def slot(i, heads, used, *_):
        return (jnp.maximum(jnp.minimum(i, used[0] - 1), 0), 0)

    return pl.pallas_call(
        retrieval_kernel,
        grid_spec=pltpu.PrefetchScalarGridSpec(
            num_scalar_prefetch=4,
            grid=(slots,),
            in_specs=[
                pl.BlockSpec((rows, D), head),
                pl.BlockSpec((rows, D), key),
                pl.BlockSpec((rows, D), value),
                pl.BlockSpec((WIN, D), key),
                pl.BlockSpec((WIN, D), value),
                pl.BlockSpec((VB * BLK, 2 * D), slot),
                pl.BlockSpec(memory_space=pl.ANY),
            ],
            out_specs=pl.BlockSpec((rows, D), head),
            scratch_shapes=[
                pltpu.VMEM((WIN + rows, D), jnp.bfloat16),
                pltpu.VMEM((WIN + rows, 2 * D), jnp.bfloat16),
                pltpu.SemaphoreType.DMA,
            ],
        ),
        out_shape=jax.ShapeDtypeStruct((rows, width), jnp.bfloat16),
        input_output_aliases={10: 0},
        compiler_params=pltpu.CompilerParams(vmem_limit_bytes=VMEM_LIMIT),
        cost_estimate=pl.CostEstimate(
            flops=4 * slots * D * rows * (VB + NSL) * BLK * 2,
            bytes_accessed=4 * rows * slots * D,
            transcendentals=slots * rows * (VB + NSL) * BLK,
        ),
        name="retrieval_heads",
    )(heads, used, counts, offsets, q, kv, kv, previous, previous, vertical, old)


def compact(flags, length):
    n = flags.shape[0]
    place = jnp.arange(n, dtype=jnp.int32)
    rank = jnp.sum(jnp.where(place[None, :] < place[:, None], flags[None, :], 0), 1)
    used = jnp.sum(flags)
    wanted = jnp.minimum(jnp.arange(length, dtype=jnp.int32), used - 1)
    hit = (rank[None, :] == wanted[:, None]) & (flags[None, :] == 1)
    return jnp.sum(jnp.where(hit, place[None, :], 0), 1).astype(jnp.int32), used


def spread(block, axis):
    size = lax.axis_size(axis)
    index = lax.axis_index(axis)
    step = size // 2
    while step >= 1:
        route = [(i, i + step) for i in range(0, size, 2 * step)]
        arrived = lax.ppermute(block, axis, route)
        block = jnp.where(lax.rem(index, 2 * step) == step, arrived, block)
        step //= 2
    return block


def exchange(block):
    return lax.all_to_all(block, "head", split_axis=1, concat_axis=0, tiled=True)


def shards(queries, keys, values, prefix_keys, prefix_values, roles, columns, col_count, diagonals):
    seq_size = lax.axis_size("seq")
    head_size = lax.axis_size("head")
    my_seq = lax.axis_index("seq")
    cache_rows, cache_width = prefix_keys.shape
    kv_count = cache_width // D
    heads_here = kv_count * SHARE
    slots = kv_count * MAX_RETRIEVERS

    finders, finder_count = compact(jnp.where(roles == 1, 1, 0), slots)
    passers, passer_count = compact(jnp.where(roles == 1, 0, 1), heads_here)
    cols = columns[finders]
    counts = col_count[finders]
    offsets = diagonals[finders].reshape(-1)
    blocks_dev = cache_rows // BLK
    used_col = (jnp.arange(VB)[None, :] < counts[:, None]) & (
        jnp.arange(slots)[:, None] < finder_count
    )
    own = ((cols // blocks_dev == my_seq) & used_col).astype(jnp.int32).reshape(-1)
    local = (cols % blocks_dev).reshape(-1)
    kv_of = jnp.broadcast_to((finders // SHARE)[:, None], (slots, VB)).reshape(-1)
    mine = collect(own, local, kv_of, prefix_keys, prefix_values)
    vertical = lax.psum(mine, "seq")

    sink = spread(jnp.concatenate([prefix_keys[:SINK], prefix_values[:SINK]], 1), "seq")
    rows_in = keys.shape[0]
    kv_out = jnp.concatenate(
        [
            keys.reshape(rows_in, head_size, cache_width),
            values.reshape(rows_in, head_size, cache_width),
        ],
        2,
    ).reshape(rows_in, head_size * 2 * cache_width)
    kv = exchange(kv_out)
    q = exchange(queries)
    tail_cache = jnp.concatenate(
        [prefix_keys[cache_rows - WIN :], prefix_values[cache_rows - WIN :]], 1
    )
    outgoing = jnp.where(my_seq == seq_size - 1, tail_cache, kv[kv.shape[0] - WIN :])
    route = [(i, (i + 1) % seq_size) for i in range(seq_size)]
    previous = lax.ppermute(outgoing, "seq", route)

    out = passing(passers, passer_count.reshape(1), q, kv, previous, sink)
    return retrieval(
        finders, finder_count.reshape(1), counts, offsets, q, kv, previous, vertical, out
    )


def solution(mesh):
    placed = (
        P(("seq", "head"), None),
        P(("seq", "head"), None),
        P(("seq", "head"), None),
        P("seq", "head"),
        P("seq", "head"),
        P("head"),
        P("head", None),
        P("head"),
        P("head", None),
    )
    return jax.shard_map(
        shards, mesh=mesh, in_specs=placed, out_specs=P("seq", "head"), check_vma=False
    )
```

```python
import functools
import math

import jax
import jax.numpy as jnp
from jax import lax
from jax.experimental import pallas as pl
from jax.experimental.pallas import tpu as pltpu
from jax.sharding import PartitionSpec as P

QUERY_HEADS = 64
KEY_VALUE_HEADS = 8
SHARE = QUERY_HEADS // KEY_VALUE_HEADS
D = 128
SINK = 128
WIN = 512
BLK = 64
VB = 6
NSL = 4
MAX_RETRIEVERS = 4
QB = 128
SCALE = math.log2(math.e) / math.sqrt(D)
VMEM_LIMIT = 40 * 1024 * 1024


def dot_nt(a, b):
    return lax.dot_general(a, b, (((1,), (1,)), ((), ())), preferred_element_type=jnp.float32)


def dot(a, b):
    return jnp.dot(a, b, preferred_element_type=jnp.float32)


def collect_kernel(own, blk, kv_of, pk, pv, out, sem, sink_sem):
    count = kv_of.shape[0]
    kv_count = pk.shape[1] // D
    out[...] = jnp.zeros_like(out)

    def copies(t):
        rows = pl.ds(pl.multiple_of(blk[t] * BLK, BLK), BLK)
        cols = pl.ds(pl.multiple_of(kv_of[t] * D, D), D)
        first = pl.ds(pl.multiple_of(t * BLK, BLK), BLK)
        second = pl.ds(pl.multiple_of((count + t) * BLK, BLK), BLK)
        return (
            pltpu.make_async_copy(pk.at[rows, cols], out.at[first, :], sem.at[0, t]),
            pltpu.make_async_copy(pv.at[rows, cols], out.at[second, :], sem.at[1, t]),
        )

    def sinks():
        base = 2 * count * BLK
        return [
            pltpu.make_async_copy(
                ref.at[pl.ds(0, SINK), pl.ds(g * D, D)],
                out.at[pl.ds(base + (part * kv_count + g) * SINK, SINK), :],
                sink_sem.at[part, g],
            )
            for part, ref in enumerate((pk, pv))
            for g in range(kv_count)
        ]

    def start(t, carry):
        @pl.when(own[t] == 1)
        def _():
            for copy in copies(t):
                copy.start()

        return carry

    def finish(t, carry):
        @pl.when(own[t] == 1)
        def _():
            for copy in copies(t):
                copy.wait()

        return carry

    @pl.when(own[count] == 1)
    def _():
        for copy in sinks():
            copy.start()

    lax.fori_loop(0, count, start, 0)
    lax.fori_loop(0, count, finish, 0)

    @pl.when(own[count] == 1)
    def _():
        for copy in sinks():
            copy.wait()


def collect(own, blk, kv_of, prefix_keys, prefix_values, rows):
    count = kv_of.shape[0]
    kv_count = prefix_keys.shape[1] // D
    return pl.pallas_call(
        collect_kernel,
        grid_spec=pltpu.PrefetchScalarGridSpec(
            num_scalar_prefetch=3,
            grid=(1,),
            in_specs=[pl.BlockSpec(memory_space=pl.ANY)] * 2,
            out_specs=pl.BlockSpec((rows, D), lambda i, *_: (0, 0)),
            scratch_shapes=[
                pltpu.SemaphoreType.DMA((2, count)),
                pltpu.SemaphoreType.DMA((2, kv_count)),
            ],
        ),
        out_shape=jax.ShapeDtypeStruct((rows, D), jnp.bfloat16),
        compiler_params=pltpu.CompilerParams(vmem_limit_bytes=VMEM_LIMIT),
        name="collect_columns",
    )(own, blk, kv_of, prefix_keys, prefix_values)


def share_kernel(size, orders, mine, out, acc, landed, send_sem, recv_sem):
    me = lax.axis_index("seq")
    bits = len(orders[0])
    barrier = pltpu.get_barrier_semaphore()

    def bit_of(b):
        return lax.rem(me // (1 << b), 2)

    def partner(b):
        return me + (1 - 2 * bit_of(b)) * (1 << b)

    for b in range(bits):
        pl.semaphore_signal(
            barrier, inc=1, device_id={"seq": partner(b)}, device_id_type=pl.DeviceIdType.MESH
        )
    pl.semaphore_wait(barrier, bits)

    streams = len(orders)
    part = mine.shape[0] // streams
    low = [part * w for w in range(streams)]
    length = [part] * streams
    started = {}

    def at(start, n):
        return pl.ds(pl.multiple_of(start, 16), n)

    def move(src, dst, w, step, b):
        copy = pltpu.make_async_remote_copy(
            src_ref=src,
            dst_ref=dst,
            send_sem=send_sem.at[w, step],
            recv_sem=recv_sem.at[w, step],
            device_id={"seq": partner(b)},
            device_id_type=pl.DeviceIdType.MESH,
        )
        copy.start()
        started[w, step] = copy

    def halve(w, step):
        b = orders[w][step]
        half = length[w] // 2
        source = mine if step == 0 else acc
        other = low[w] + (1 - bit_of(b)) * half
        place = part * w + part - length[w]
        move(source.at[at(other, half), :], landed.at[pl.ds(place, half), :], w, step, b)

    def add(w, step):
        b = orders[w][step]
        half = length[w] // 2
        source = mine if step == 0 else acc
        place = part * w + part - length[w]
        keep = at(low[w] + bit_of(b) * half, half)
        started[w, step].wait()
        into = out if step == bits - 1 else acc
        into[keep, :] = source[keep, :] + landed[pl.ds(place, half), :]
        low[w] = low[w] + bit_of(b) * half
        length[w] = half

    def double(w, step):
        b = orders[w][2 * bits - 1 - step]
        whole = out.at[at(low[w], length[w]), :]
        move(whole, whole, w, step, b)

    def join(w, step):
        b = orders[w][2 * bits - 1 - step]
        started[w, step].wait()
        low[w] = low[w] - bit_of(b) * length[w]
        length[w] = 2 * length[w]

    for step in range(2 * bits + 1):
        for w in range(streams):
            if 0 < step <= bits:
                add(w, step - 1)
            elif step > bits:
                join(w, step - 1)
            if step < bits:
                halve(w, step)
            elif step < 2 * bits:
                double(w, step)


def share(mine):
    size = lax.axis_size("seq")
    bits = size.bit_length() - 1
    orders = [list(range(bits)), [0, *range(2, bits), 1]]
    rows = mine.shape[0]
    return pl.pallas_call(
        functools.partial(share_kernel, size, orders),
        out_shape=jax.ShapeDtypeStruct(mine.shape, mine.dtype),
        in_specs=[pl.BlockSpec(memory_space=pltpu.VMEM)],
        out_specs=pl.BlockSpec(memory_space=pltpu.VMEM),
        scratch_shapes=[
            pltpu.VMEM((rows, D), mine.dtype),
            pltpu.VMEM((rows, D), mine.dtype),
            pltpu.SemaphoreType.DMA((len(orders), 2 * bits)),
            pltpu.SemaphoreType.DMA((len(orders), 2 * bits)),
        ],
        compiler_params=pltpu.CompilerParams(
            collective_id=0, has_side_effects=True, vmem_limit_bytes=VMEM_LIMIT
        ),
        cost_estimate=pl.CostEstimate(
            flops=10**10, bytes_accessed=8 * rows * D, transcendentals=0
        ),
        name="share_columns",
    )(mine)


def new_group(heads, i):
    before = heads[jnp.maximum(i - 1, 0)]
    return (i == 0) | (heads[i] // SHARE != before // SHARE)


def passing_kernel(heads, used, q, k, v, pk, pv, sk, sv, out, keys_t, vals):
    i = pl.program_id(0)
    rows = q.shape[0]

    @pl.when(new_group(heads, i))
    def _():
        keys_t[:, :SINK] = sk[...].T
        keys_t[:, SINK : SINK + WIN] = pk[...].T
        keys_t[:, SINK + WIN :] = k[...].T
        vals[:SINK, :D] = sv[...]
        vals[SINK : SINK + WIN, :D] = pv[...]
        vals[SINK + WIN :, :D] = v[...]
        vals[:, D:] = jnp.ones_like(vals[:, D:])

    @pl.when(i < used[0])
    def _():
        row = lax.broadcasted_iota(jnp.int32, (QB, QB), 0)
        col = lax.broadcasted_iota(jnp.int32, (QB, QB), 1)
        for r in range(0, rows, QB):
            low, high = SINK + r, SINK + r + WIN + QB
            window = jnp.concatenate([keys_t[:, :SINK], keys_t[:, low:high]], 1)
            s = dot(q[r : r + QB, :], window)
            s = jnp.concatenate(
                [
                    s[:, :SINK],
                    jnp.where(col > row, s[:, SINK : SINK + QB], -jnp.inf),
                    s[:, SINK + QB : SINK + WIN],
                    jnp.where(col <= row, s[:, SINK + WIN :], -jnp.inf),
                ],
                1,
            )
            top = jnp.max(s, axis=1, keepdims=True)
            p = jnp.exp2((s - top) * SCALE).astype(jnp.bfloat16)
            acc = dot(p, jnp.concatenate([vals[:SINK, :], vals[low:high, :]], 0))
            out[r : r + QB, :] = (acc[:, :D] / acc[:, D:]).astype(out.dtype)


def passing(heads, used, q, kv, previous, shared, sink_block):
    rows, width = q.shape
    kv_count = kv.shape[1] // (2 * D)

    def sink_key(i, heads, used):
        return (sink_block + heads[i] // SHARE, 0)

    def sink_value(i, heads, used):
        return (sink_block + kv_count + heads[i] // SHARE, 0)

    def head(i, heads, used):
        return (0, heads[i])

    def key(i, heads, used):
        return (0, heads[i] // SHARE)

    def value(i, heads, used):
        return (0, kv_count + heads[i] // SHARE)

    return pl.pallas_call(
        passing_kernel,
        grid_spec=pltpu.PrefetchScalarGridSpec(
            num_scalar_prefetch=2,
            grid=(heads.shape[0],),
            in_specs=[
                pl.BlockSpec((rows, D), head),
                pl.BlockSpec((rows, D), key),
                pl.BlockSpec((rows, D), value),
                pl.BlockSpec((WIN, D), key),
                pl.BlockSpec((WIN, D), value),
                pl.BlockSpec((SINK, D), sink_key),
                pl.BlockSpec((SINK, D), sink_value),
            ],
            out_specs=pl.BlockSpec((rows, D), head),
            scratch_shapes=[
                pltpu.VMEM((D, SINK + WIN + rows), jnp.bfloat16),
                pltpu.VMEM((SINK + WIN + rows, 2 * D), jnp.bfloat16),
            ],
        ),
        out_shape=jax.ShapeDtypeStruct((rows, width), jnp.bfloat16),
        compiler_params=pltpu.CompilerParams(vmem_limit_bytes=VMEM_LIMIT),
        cost_estimate=pl.CostEstimate(
            flops=4 * width * rows * (SINK + WIN + QB) * 2,
            bytes_accessed=4 * rows * width,
            transcendentals=width // D * rows * (SINK + WIN + QB),
        ),
        name="passing_heads",
    )(heads, used, q, kv, kv, previous, previous, shared, shared)


def retrieval_kernel(
    heads, used, counts, offsets, q, k, v, pk, pv, far_k, far_v, old, out, keys, vals, sem
):
    i = pl.program_id(0)
    rows = q.shape[0]

    @pl.when(new_group(heads, i))
    def _():
        keys[:WIN, :] = pk[...]
        keys[WIN:, :] = k[...]
        vals[:WIN, :D] = pv[...]
        vals[WIN:, :D] = v[...]
        vals[:, D:] = jnp.ones_like(vals[:, D:])

    @pl.when((i == 0) & (used[0] == 0))
    def _():
        copy = pltpu.make_async_copy(old.at[:, pl.ds(0, D)], out, sem)
        copy.start()
        copy.wait()

    @pl.when(i < used[0])
    def _():
        row = lax.broadcasted_iota(jnp.int32, (BLK, NSL * BLK), 0)
        col = lax.broadcasted_iota(jnp.int32, (BLK, NSL * BLK), 1)
        causal = (col <= row) | (col >= BLK)
        lane = lax.broadcasted_iota(jnp.int32, (1, VB * BLK), 1)
        open_cols = lane < counts[i] * BLK
        vert_k = far_k[...]
        vert_v = jnp.concatenate([far_v[...], jnp.ones((VB * BLK, D), jnp.bfloat16)], 1)
        for r in range(0, rows, QB):
            q_rows = q[r : r + QB, :]
            s_vert = jnp.where(open_cols, dot_nt(q_rows, vert_k), -jnp.inf)
            p_verts, slashes = [], []
            for b in range(0, QB, BLK):
                picks = [
                    pl.ds(
                        pl.multiple_of((WIN + r + b) - offsets[i * NSL + t] * BLK, BLK), BLK
                    )
                    for t in range(NSL)
                ]
                near_k = jnp.concatenate([keys[pick, :] for pick in picks], 0)
                near_v = jnp.concatenate([vals[pick, :] for pick in picks], 0)
                s_near = jnp.where(causal, dot_nt(q_rows[b : b + BLK], near_k), -jnp.inf)
                s_far = s_vert[b : b + BLK]
                top = jnp.maximum(
                    jnp.max(s_near, axis=1, keepdims=True), jnp.max(s_far, axis=1, keepdims=True)
                )
                p_near = jnp.exp2((s_near - top) * SCALE).astype(jnp.bfloat16)
                p_verts.append(jnp.exp2((s_far - top) * SCALE).astype(jnp.bfloat16))
                slashes.append(dot(p_near, near_v))
            acc = dot(jnp.concatenate(p_verts, 0), vert_v) + jnp.concatenate(slashes, 0)
            out[r : r + QB, :] = (acc[:, :D] / acc[:, D:]).astype(out.dtype)


def retrieval(heads, used, counts, offsets, q, kv, previous, shared, old):
    rows, width = q.shape
    kv_count = kv.shape[1] // (2 * D)
    slots = heads.shape[0]

    def head(i, heads, *_):
        return (0, heads[i])

    def key(i, heads, *_):
        return (0, heads[i] // SHARE)

    def value(i, heads, *_):
        return (0, kv_count + heads[i] // SHARE)

    def slot(i, heads, used, *_):
        return (jnp.maximum(jnp.minimum(i, used[0] - 1), 0), 0)

    def slot_value(i, heads, used, *_):
        return (slots + jnp.maximum(jnp.minimum(i, used[0] - 1), 0), 0)

    return pl.pallas_call(
        retrieval_kernel,
        grid_spec=pltpu.PrefetchScalarGridSpec(
            num_scalar_prefetch=4,
            grid=(slots,),
            in_specs=[
                pl.BlockSpec((rows, D), head),
                pl.BlockSpec((rows, D), key),
                pl.BlockSpec((rows, D), value),
                pl.BlockSpec((WIN, D), key),
                pl.BlockSpec((WIN, D), value),
                pl.BlockSpec((VB * BLK, D), slot),
                pl.BlockSpec((VB * BLK, D), slot_value),
                pl.BlockSpec(memory_space=pl.ANY),
            ],
            out_specs=pl.BlockSpec((rows, D), head),
            scratch_shapes=[
                pltpu.VMEM((WIN + rows, D), jnp.bfloat16),
                pltpu.VMEM((WIN + rows, 2 * D), jnp.bfloat16),
                pltpu.SemaphoreType.DMA,
            ],
        ),
        out_shape=jax.ShapeDtypeStruct((rows, width), jnp.bfloat16),
        input_output_aliases={11: 0},
        compiler_params=pltpu.CompilerParams(vmem_limit_bytes=VMEM_LIMIT),
        cost_estimate=pl.CostEstimate(
            flops=4 * slots * D * rows * (VB + NSL) * BLK * 2,
            bytes_accessed=4 * rows * slots * D,
            transcendentals=slots * rows * (VB + NSL) * BLK,
        ),
        name="retrieval_heads",
    )(heads, used, counts, offsets, q, kv, kv, previous, previous, shared, shared, old)


def compact(flags, length):
    n = flags.shape[0]
    place = jnp.arange(n, dtype=jnp.int32)
    rank = jnp.sum(jnp.where(place[None, :] < place[:, None], flags[None, :], 0), 1)
    used = jnp.sum(flags)
    wanted = jnp.minimum(jnp.arange(length, dtype=jnp.int32), used - 1)
    hit = (rank[None, :] == wanted[:, None]) & (flags[None, :] == 1)
    return jnp.sum(jnp.where(hit, place[None, :], 0), 1).astype(jnp.int32), used


def exchange(block):
    return lax.all_to_all(block, "head", split_axis=1, concat_axis=0, tiled=True)


def shards(queries, keys, values, prefix_keys, prefix_values, roles, columns, col_count, diagonals):
    seq_size = lax.axis_size("seq")
    head_size = lax.axis_size("head")
    my_seq = lax.axis_index("seq")
    cache_rows, cache_width = prefix_keys.shape
    kv_count = cache_width // D
    heads_here = kv_count * SHARE
    slots = kv_count * MAX_RETRIEVERS

    finders, finder_count = compact(jnp.where(roles == 1, 1, 0), slots)
    passers, passer_count = compact(jnp.where(roles == 1, 0, 1), heads_here)
    cols = columns[finders]
    counts = col_count[finders]
    offsets = diagonals[finders].reshape(-1)
    blocks_dev = cache_rows // BLK
    used_col = (jnp.arange(VB)[None, :] < counts[:, None]) & (
        jnp.arange(slots)[:, None] < finder_count
    )
    own = ((cols // blocks_dev == my_seq) & used_col).astype(jnp.int32).reshape(-1)
    local = (cols % blocks_dev).reshape(-1)
    kv_of = jnp.broadcast_to((finders // SHARE)[:, None], (slots, VB)).reshape(-1)
    own = jnp.concatenate([own, (my_seq == 0).astype(jnp.int32).reshape(1)])
    sink_at = 2 * slots * VB * BLK
    unit = 2 * 16 * seq_size
    shared_rows = -(-(sink_at + 2 * kv_count * SINK) // unit) * unit
    mine = collect(own, local, kv_of, prefix_keys, prefix_values, shared_rows)
    shared = share(mine)

    rows_in = keys.shape[0]
    kv_out = jnp.concatenate(
        [
            keys.reshape(rows_in, head_size, cache_width),
            values.reshape(rows_in, head_size, cache_width),
        ],
        2,
    ).reshape(rows_in, head_size * 2 * cache_width)
    kv = exchange(kv_out)
    q = exchange(queries)
    tail_cache = jnp.concatenate(
        [prefix_keys[cache_rows - WIN :], prefix_values[cache_rows - WIN :]], 1
    )
    outgoing = jnp.where(my_seq == seq_size - 1, tail_cache, kv[kv.shape[0] - WIN :])
    route = [(i, (i + 1) % seq_size) for i in range(seq_size)]
    previous = lax.ppermute(outgoing, "seq", route)

    out = passing(passers, passer_count.reshape(1), q, kv, previous, shared, sink_at // SINK)
    return retrieval(
        finders, finder_count.reshape(1), counts, offsets, q, kv, previous, shared, out
    )


def solution(mesh):
    placed = (
        P(("seq", "head"), None),
        P(("seq", "head"), None),
        P(("seq", "head"), None),
        P("seq", "head"),
        P("seq", "head"),
        P("head"),
        P("head", None),
        P("head"),
        P("head", None),
    )
    return jax.shard_map(
        shards, mesh=mesh, in_specs=placed, out_specs=P("seq", "head"), check_vma=False
    )
```

```python
import functools
import math

import jax
import jax.numpy as jnp
from jax import lax
from jax.experimental import pallas as pl
from jax.experimental.pallas import tpu as pltpu
from jax.sharding import PartitionSpec as P

QUERY_HEADS = 64
KEY_VALUE_HEADS = 8
SHARE = QUERY_HEADS // KEY_VALUE_HEADS
D = 128
SINK = 128
WIN = 512
BLK = 64
VB = 6
NSL = 4
MAX_RETRIEVERS = 4
QB = 128
SCALE = math.log2(math.e) / math.sqrt(D)
VMEM_LIMIT = 40 * 1024 * 1024


def dot_nt(a, b):
    return lax.dot_general(a, b, (((1,), (1,)), ((), ())), preferred_element_type=jnp.float32)


def dot(a, b):
    return jnp.dot(a, b, preferred_element_type=jnp.float32)


def collect_kernel(own, blk, kv_of, pk, pv, out, sem, sink_sem):
    count = kv_of.shape[0]
    kv_count = pk.shape[1] // D
    out[...] = jnp.zeros_like(out)

    def copies(t):
        rows = pl.ds(pl.multiple_of(blk[t] * BLK, BLK), BLK)
        cols = pl.ds(pl.multiple_of(kv_of[t] * D, D), D)
        first = pl.ds(pl.multiple_of(t * BLK, BLK), BLK)
        second = pl.ds(pl.multiple_of((count + t) * BLK, BLK), BLK)
        return (
            pltpu.make_async_copy(pk.at[rows, cols], out.at[first, :], sem.at[0, t]),
            pltpu.make_async_copy(pv.at[rows, cols], out.at[second, :], sem.at[1, t]),
        )

    def sinks():
        base = 2 * count * BLK
        return [
            pltpu.make_async_copy(
                ref.at[pl.ds(0, SINK), pl.ds(g * D, D)],
                out.at[pl.ds(base + (part * kv_count + g) * SINK, SINK), :],
                sink_sem.at[part, g],
            )
            for part, ref in enumerate((pk, pv))
            for g in range(kv_count)
        ]

    def start(t, carry):
        @pl.when(own[t] == 1)
        def _():
            for copy in copies(t):
                copy.start()

        return carry

    def finish(t, carry):
        @pl.when(own[t] == 1)
        def _():
            for copy in copies(t):
                copy.wait()

        return carry

    @pl.when(own[count] == 1)
    def _():
        for copy in sinks():
            copy.start()

    lax.fori_loop(0, count, start, 0)
    lax.fori_loop(0, count, finish, 0)

    @pl.when(own[count] == 1)
    def _():
        for copy in sinks():
            copy.wait()


def collect(own, blk, kv_of, prefix_keys, prefix_values, rows):
    count = kv_of.shape[0]
    kv_count = prefix_keys.shape[1] // D
    return pl.pallas_call(
        collect_kernel,
        grid_spec=pltpu.PrefetchScalarGridSpec(
            num_scalar_prefetch=3,
            grid=(1,),
            in_specs=[pl.BlockSpec(memory_space=pltpu.HBM)] * 2,
            out_specs=pl.BlockSpec((rows, D), lambda i, *_: (0, 0)),
            scratch_shapes=[
                pltpu.SemaphoreType.DMA((2, count)),
                pltpu.SemaphoreType.DMA((2, kv_count)),
            ],
        ),
        out_shape=jax.ShapeDtypeStruct((rows, D), jnp.bfloat16),
        compiler_params=pltpu.CompilerParams(vmem_limit_bytes=VMEM_LIMIT),
        name="collect_columns",
    )(own, blk, kv_of, prefix_keys, prefix_values)


def share_kernel(
    size,
    heads,
    orders,
    mine,
    queries,
    keys,
    values,
    cache_k,
    cache_v,
    out,
    q_out,
    kv_out,
    previous,
    acc,
    landed,
    send_sem,
    recv_sem,
    swap_send,
    swap_recv,
    tail_send,
    tail_recv,
    own_sem,
):
    me = lax.axis_index("seq")
    my_head = lax.axis_index("head")
    right, left = lax.rem(me + 1, size), lax.rem(me + size - 1, size)
    bits = len(orders[0])
    barrier = pltpu.get_barrier_semaphore()

    def bit_of(b):
        return lax.rem(me // (1 << b), 2)

    def partner(b):
        return me + (1 - 2 * bit_of(b)) * (1 << b)

    for b in range(bits):
        pl.semaphore_signal(
            barrier, inc=1, device_id={"seq": partner(b)}, device_id_type=pl.DeviceIdType.MESH
        )
    for d in range(1, heads):
        pl.semaphore_signal(
            barrier,
            inc=1,
            device_id={"head": lax.rem(my_head + d, heads)},
            device_id_type=pl.DeviceIdType.MESH,
        )
    for neighbour in (left, right):
        pl.semaphore_signal(
            barrier, inc=1, device_id={"seq": neighbour}, device_id_type=pl.DeviceIdType.MESH
        )
    pl.semaphore_wait(barrier, bits + heads + 1)

    rows_in, cache_width = keys.shape[0], cache_k.shape[1]
    my_rows = pl.ds(pl.multiple_of(my_head * rows_in, 16), rows_in)
    swaps = (
        (keys, kv_out.at[my_rows, pl.ds(0, cache_width)], cache_width),
        (values, kv_out.at[my_rows, pl.ds(cache_width, cache_width)], cache_width),
        (queries, q_out.at[my_rows, :], q_out.shape[1]),
    )
    swapped = []
    for n, (source, target, width) in enumerate(swaps):
        row = []
        for d in range(heads):
            to = lax.rem(my_head + d, heads)
            block = source.at[:, pl.ds(pl.multiple_of(to * width, D), width)]
            if d == 0:
                copy = pltpu.make_async_copy(block, target, own_sem.at[n])
            else:
                copy = pltpu.make_async_remote_copy(
                    src_ref=block,
                    dst_ref=target,
                    send_sem=swap_send.at[n, d - 1],
                    recv_sem=swap_recv.at[n, d - 1],
                    device_id={"head": to},
                    device_id_type=pl.DeviceIdType.MESH,
                )
            copy.start()
            row.append(copy)
        swapped.append(row)

    def tails(cached):
        copies = []
        for n, cache in enumerate((cache_k, cache_v)):
            place = pl.ds(n * cache_width, cache_width)
            if cached:
                source = cache.at[pl.ds(cache.shape[0] - WIN, WIN), :]
            else:
                source = kv_out.at[pl.ds(kv_out.shape[0] - WIN, WIN), place]
            copies.append(
                pltpu.make_async_remote_copy(
                    src_ref=source,
                    dst_ref=previous.at[:, place],
                    send_sem=tail_send.at[n],
                    recv_sem=tail_recv.at[n],
                    device_id={"seq": right},
                    device_id_type=pl.DeviceIdType.MESH,
                )
            )
        return copies

    def pass_tails():
        for row in swapped[:2]:
            for copy in row:
                copy.wait()

        @pl.when(me == size - 1)
        def _():
            for copy in tails(True):
                copy.start()

        @pl.when(me != size - 1)
        def _():
            for copy in tails(False):
                copy.start()

    streams = len(orders)
    part = mine.shape[0] // streams
    low = [part * w for w in range(streams)]
    length = [part] * streams
    started = {}

    def at(start, n):
        return pl.ds(pl.multiple_of(start, 16), n)

    def move(src, dst, w, step, b):
        copy = pltpu.make_async_remote_copy(
            src_ref=src,
            dst_ref=dst,
            send_sem=send_sem.at[w, step],
            recv_sem=recv_sem.at[w, step],
            device_id={"seq": partner(b)},
            device_id_type=pl.DeviceIdType.MESH,
        )
        copy.start()
        started[w, step] = copy

    def halve(w, step):
        b = orders[w][step]
        half = length[w] // 2
        source = mine if step == 0 else acc
        other = low[w] + (1 - bit_of(b)) * half
        place = part * w + part - length[w]
        move(source.at[at(other, half), :], landed.at[pl.ds(place, half), :], w, step, b)

    def add(w, step):
        b = orders[w][step]
        half = length[w] // 2
        source = mine if step == 0 else acc
        place = part * w + part - length[w]
        keep = at(low[w] + bit_of(b) * half, half)
        started[w, step].wait()
        into = out if step == bits - 1 else acc
        into[keep, :] = source[keep, :] + landed[pl.ds(place, half), :]
        low[w] = low[w] + bit_of(b) * half
        length[w] = half

    def double(w, step):
        b = orders[w][2 * bits - 1 - step]
        whole = out.at[at(low[w], length[w]), :]
        move(whole, whole, w, step, b)

    def join(w, step):
        b = orders[w][2 * bits - 1 - step]
        started[w, step].wait()
        low[w] = low[w] - bit_of(b) * length[w]
        length[w] = 2 * length[w]

    for step in range(2 * bits + 1):
        for w in range(streams):
            if 0 < step <= bits:
                add(w, step - 1)
            elif step > bits:
                join(w, step - 1)
            if step < bits:
                halve(w, step)
            elif step < 2 * bits:
                double(w, step)
        if step == 1:
            pass_tails()
    for copy in tails(False):
        copy.wait()
    for copy in swapped[2]:
        copy.wait()


def share(mine, queries, keys, values, prefix_keys, prefix_values):
    size, heads = lax.axis_size("seq"), lax.axis_size("head")
    bits = size.bit_length() - 1
    orders = [list(range(bits)), [0, *range(2, bits), 1]]
    rows = mine.shape[0]
    kind = mine.dtype
    span = keys.shape[0] * heads
    cache_width = prefix_keys.shape[1]
    anywhere = pl.BlockSpec(memory_space=pltpu.HBM)
    local = pl.BlockSpec(memory_space=pltpu.VMEM)
    return pl.pallas_call(
        functools.partial(share_kernel, size, heads, orders),
        out_shape=(
            jax.ShapeDtypeStruct(mine.shape, kind),
            jax.ShapeDtypeStruct((span, queries.shape[1] // heads), kind),
            jax.ShapeDtypeStruct((span, 2 * cache_width), kind),
            jax.ShapeDtypeStruct((WIN, 2 * cache_width), kind),
        ),
        in_specs=[local] + [anywhere] * 5,
        out_specs=(local, anywhere, anywhere, anywhere),
        scratch_shapes=[
            pltpu.VMEM((rows, D), kind),
            pltpu.VMEM((rows, D), kind),
            pltpu.SemaphoreType.DMA((len(orders), 2 * bits)),
            pltpu.SemaphoreType.DMA((len(orders), 2 * bits)),
            pltpu.SemaphoreType.DMA((3, heads - 1)),
            pltpu.SemaphoreType.DMA((3, heads - 1)),
            pltpu.SemaphoreType.DMA((2,)),
            pltpu.SemaphoreType.DMA((2,)),
            pltpu.SemaphoreType.DMA((3,)),
        ],
        compiler_params=pltpu.CompilerParams(
            collective_id=0, has_side_effects=True, vmem_limit_bytes=VMEM_LIMIT
        ),
        cost_estimate=pl.CostEstimate(
            flops=10**10, bytes_accessed=8 * rows * D, transcendentals=0
        ),
        name="share_columns",
    )(mine, queries, keys, values, prefix_keys, prefix_values)


def new_group(heads, i):
    before = heads[jnp.maximum(i - 1, 0)]
    return (i == 0) | (heads[i] // SHARE != before // SHARE)


def passing_kernel(heads, used, q, k, v, pk, pv, sk, sv, out, keys_t, vals):
    i = pl.program_id(0)
    rows = q.shape[0]

    @pl.when(new_group(heads, i))
    def _():
        keys_t[:, :SINK] = sk[...].T
        keys_t[:, SINK : SINK + WIN] = pk[...].T
        keys_t[:, SINK + WIN :] = k[...].T
        vals[:SINK, :D] = sv[...]
        vals[SINK : SINK + WIN, :D] = pv[...]
        vals[SINK + WIN :, :D] = v[...]
        vals[:, D:] = jnp.ones_like(vals[:, D:])

    @pl.when(i < used[0])
    def _():
        row = lax.broadcasted_iota(jnp.int32, (QB, QB), 0)
        col = lax.broadcasted_iota(jnp.int32, (QB, QB), 1)
        for r in range(0, rows, QB):
            low, high = SINK + r, SINK + r + WIN + QB
            window = jnp.concatenate([keys_t[:, :SINK], keys_t[:, low:high]], 1)
            s = dot(q[r : r + QB, :], window)
            s = jnp.concatenate(
                [
                    s[:, :SINK],
                    jnp.where(col > row, s[:, SINK : SINK + QB], -jnp.inf),
                    s[:, SINK + QB : SINK + WIN],
                    jnp.where(col <= row, s[:, SINK + WIN :], -jnp.inf),
                ],
                1,
            )
            top = jnp.max(s, axis=1, keepdims=True)
            p = jnp.exp2((s - top) * SCALE).astype(jnp.bfloat16)
            acc = dot(p, jnp.concatenate([vals[:SINK, :], vals[low:high, :]], 0))
            out[r : r + QB, :] = (acc[:, :D] / acc[:, D:]).astype(out.dtype)


def passing(heads, used, q, kv, previous, shared, sink_block):
    rows, width = q.shape
    kv_count = kv.shape[1] // (2 * D)

    def sink_key(i, heads, used):
        return (sink_block + heads[i] // SHARE, 0)

    def sink_value(i, heads, used):
        return (sink_block + kv_count + heads[i] // SHARE, 0)

    def head(i, heads, used):
        return (0, heads[i])

    def key(i, heads, used):
        return (0, heads[i] // SHARE)

    def value(i, heads, used):
        return (0, kv_count + heads[i] // SHARE)

    return pl.pallas_call(
        passing_kernel,
        grid_spec=pltpu.PrefetchScalarGridSpec(
            num_scalar_prefetch=2,
            grid=(heads.shape[0],),
            in_specs=[
                pl.BlockSpec((rows, D), head),
                pl.BlockSpec((rows, D), key),
                pl.BlockSpec((rows, D), value),
                pl.BlockSpec((WIN, D), key),
                pl.BlockSpec((WIN, D), value),
                pl.BlockSpec((SINK, D), sink_key),
                pl.BlockSpec((SINK, D), sink_value),
            ],
            out_specs=pl.BlockSpec((rows, D), head),
            scratch_shapes=[
                pltpu.VMEM((D, SINK + WIN + rows), jnp.bfloat16),
                pltpu.VMEM((SINK + WIN + rows, 2 * D), jnp.bfloat16),
            ],
        ),
        out_shape=jax.ShapeDtypeStruct((rows, width), jnp.bfloat16),
        compiler_params=pltpu.CompilerParams(vmem_limit_bytes=VMEM_LIMIT),
        cost_estimate=pl.CostEstimate(
            flops=4 * width * rows * (SINK + WIN + QB) * 2,
            bytes_accessed=4 * rows * width,
            transcendentals=width // D * rows * (SINK + WIN + QB),
        ),
        name="passing_heads",
    )(heads, used, q, kv, kv, previous, previous, shared, shared)


def retrieval_kernel(
    heads, used, counts, offsets, q, k, v, pk, pv, far_k, far_v, old, out, keys, vals, sem
):
    i = pl.program_id(0)
    rows = q.shape[0]

    @pl.when(new_group(heads, i))
    def _():
        keys[:WIN, :] = pk[...]
        keys[WIN:, :] = k[...]
        vals[:WIN, :D] = pv[...]
        vals[WIN:, :D] = v[...]
        vals[:, D:] = jnp.ones_like(vals[:, D:])

    @pl.when((i == 0) & (used[0] == 0))
    def _():
        copy = pltpu.make_async_copy(old.at[:, pl.ds(0, D)], out, sem)
        copy.start()
        copy.wait()

    @pl.when(i < used[0])
    def _():
        row = lax.broadcasted_iota(jnp.int32, (BLK, NSL * BLK), 0)
        col = lax.broadcasted_iota(jnp.int32, (BLK, NSL * BLK), 1)
        causal = (col <= row) | (col >= BLK)
        lane = lax.broadcasted_iota(jnp.int32, (1, VB * BLK), 1)
        open_cols = lane < counts[i] * BLK
        vert_k = far_k[...]
        vert_v = jnp.concatenate([far_v[...], jnp.ones((VB * BLK, D), jnp.bfloat16)], 1)
        for r in range(0, rows, QB):
            q_rows = q[r : r + QB, :]
            s_vert = jnp.where(open_cols, dot_nt(q_rows, vert_k), -jnp.inf)
            p_verts, slashes = [], []
            for b in range(0, QB, BLK):
                picks = [
                    pl.ds(
                        pl.multiple_of((WIN + r + b) - offsets[i * NSL + t] * BLK, BLK), BLK
                    )
                    for t in range(NSL)
                ]
                near_k = jnp.concatenate([keys[pick, :] for pick in picks], 0)
                near_v = jnp.concatenate([vals[pick, :] for pick in picks], 0)
                s_near = jnp.where(causal, dot_nt(q_rows[b : b + BLK], near_k), -jnp.inf)
                s_far = s_vert[b : b + BLK]
                top = jnp.maximum(
                    jnp.max(s_near, axis=1, keepdims=True), jnp.max(s_far, axis=1, keepdims=True)
                )
                p_near = jnp.exp2((s_near - top) * SCALE).astype(jnp.bfloat16)
                p_verts.append(jnp.exp2((s_far - top) * SCALE).astype(jnp.bfloat16))
                slashes.append(dot(p_near, near_v))
            acc = dot(jnp.concatenate(p_verts, 0), vert_v) + jnp.concatenate(slashes, 0)
            out[r : r + QB, :] = (acc[:, :D] / acc[:, D:]).astype(out.dtype)


def retrieval(heads, used, counts, offsets, q, kv, previous, shared, old):
    rows, width = q.shape
    kv_count = kv.shape[1] // (2 * D)
    slots = heads.shape[0]

    def head(i, heads, *_):
        return (0, heads[i])

    def key(i, heads, *_):
        return (0, heads[i] // SHARE)

    def value(i, heads, *_):
        return (0, kv_count + heads[i] // SHARE)

    def slot(i, heads, used, *_):
        return (jnp.maximum(jnp.minimum(i, used[0] - 1), 0), 0)

    def slot_value(i, heads, used, *_):
        return (slots + jnp.maximum(jnp.minimum(i, used[0] - 1), 0), 0)

    return pl.pallas_call(
        retrieval_kernel,
        grid_spec=pltpu.PrefetchScalarGridSpec(
            num_scalar_prefetch=4,
            grid=(slots,),
            in_specs=[
                pl.BlockSpec((rows, D), head),
                pl.BlockSpec((rows, D), key),
                pl.BlockSpec((rows, D), value),
                pl.BlockSpec((WIN, D), key),
                pl.BlockSpec((WIN, D), value),
                pl.BlockSpec((VB * BLK, D), slot),
                pl.BlockSpec((VB * BLK, D), slot_value),
                pl.BlockSpec(memory_space=pl.ANY),
            ],
            out_specs=pl.BlockSpec((rows, D), head),
            scratch_shapes=[
                pltpu.VMEM((WIN + rows, D), jnp.bfloat16),
                pltpu.VMEM((WIN + rows, 2 * D), jnp.bfloat16),
                pltpu.SemaphoreType.DMA,
            ],
        ),
        out_shape=jax.ShapeDtypeStruct((rows, width), jnp.bfloat16),
        input_output_aliases={11: 0},
        compiler_params=pltpu.CompilerParams(vmem_limit_bytes=VMEM_LIMIT),
        cost_estimate=pl.CostEstimate(
            flops=4 * slots * D * rows * (VB + NSL) * BLK * 2,
            bytes_accessed=4 * rows * slots * D,
            transcendentals=slots * rows * (VB + NSL) * BLK,
        ),
        name="retrieval_heads",
    )(heads, used, counts, offsets, q, kv, kv, previous, previous, shared, shared, old)


def compact(flags, length):
    n = flags.shape[0]
    place = jnp.arange(n, dtype=jnp.int32)
    rank = jnp.sum(jnp.where(place[None, :] < place[:, None], flags[None, :], 0), 1)
    used = jnp.sum(flags)
    wanted = jnp.minimum(jnp.arange(length, dtype=jnp.int32), used - 1)
    hit = (rank[None, :] == wanted[:, None]) & (flags[None, :] == 1)
    return jnp.sum(jnp.where(hit, place[None, :], 0), 1).astype(jnp.int32), used


def shards(queries, keys, values, prefix_keys, prefix_values, roles, columns, col_count, diagonals):
    seq_size = lax.axis_size("seq")
    my_seq = lax.axis_index("seq")
    cache_rows, cache_width = prefix_keys.shape
    kv_count = cache_width // D
    heads_here = kv_count * SHARE
    slots = kv_count * MAX_RETRIEVERS

    finders, finder_count = compact(jnp.where(roles == 1, 1, 0), slots)
    passers, passer_count = compact(jnp.where(roles == 1, 0, 1), heads_here)
    cols = columns[finders]
    counts = col_count[finders]
    offsets = diagonals[finders].reshape(-1)
    blocks_dev = cache_rows // BLK
    used_col = (jnp.arange(VB)[None, :] < counts[:, None]) & (
        jnp.arange(slots)[:, None] < finder_count
    )
    own = ((cols // blocks_dev == my_seq) & used_col).astype(jnp.int32).reshape(-1)
    local = (cols % blocks_dev).reshape(-1)
    kv_of = jnp.broadcast_to((finders // SHARE)[:, None], (slots, VB)).reshape(-1)
    own = jnp.concatenate([own, (my_seq == 0).astype(jnp.int32).reshape(1)])
    sink_at = 2 * slots * VB * BLK
    unit = 2 * 16 * seq_size
    shared_rows = -(-(sink_at + 2 * kv_count * SINK) // unit) * unit
    mine = collect(own, local, kv_of, prefix_keys, prefix_values, shared_rows)
    shared, q, kv, previous = share(
        mine, queries, keys, values, prefix_keys, prefix_values
    )
    out = passing(passers, passer_count.reshape(1), q, kv, previous, shared, sink_at // SINK)
    return retrieval(
        finders, finder_count.reshape(1), counts, offsets, q, kv, previous, shared, out
    )


def solution(mesh):
    placed = (
        P(("seq", "head"), None),
        P(("seq", "head"), None),
        P(("seq", "head"), None),
        P("seq", "head"),
        P("seq", "head"),
        P("head"),
        P("head", None),
        P("head"),
        P("head", None),
    )
    return jax.shard_map(
        shards, mesh=mesh, in_specs=placed, out_specs=P("seq", "head"), check_vma=False
    )
```

```python
import functools
import math

import jax
import jax.numpy as jnp
from jax import lax
from jax.experimental import pallas as pl
from jax.experimental.pallas import tpu as pltpu
from jax.sharding import PartitionSpec as P

QUERY_HEADS = 64
KEY_VALUE_HEADS = 8
SHARE = QUERY_HEADS // KEY_VALUE_HEADS
D = 128
SINK = 128
WIN = 512
BLK = 64
VB = 6
NSL = 4
MAX_RETRIEVERS = 4
QB = 128
SCALE = math.log2(math.e) / math.sqrt(D)
VMEM_LIMIT = 40 * 1024 * 1024


def dot_nt(a, b):
    return lax.dot_general(a, b, (((1,), (1,)), ((), ())), preferred_element_type=jnp.float32)


def dot(a, b):
    return jnp.dot(a, b, preferred_element_type=jnp.float32)


def collect_kernel(seq, roles, columns, col_count, pk, pv, out, sem, sink_sem):
    blocks_dev = pk.shape[0] // BLK
    kv_count = pk.shape[1] // D
    slots = kv_count * MAX_RETRIEVERS
    out[...] = jnp.zeros_like(out)

    def copies(head, slot, c, col):
        local = col - seq[0] * blocks_dev
        rows = pl.ds(pl.multiple_of(local * BLK, BLK), BLK)
        cols = pl.ds(pl.multiple_of((head // SHARE) * D, D), D)
        t = slot * VB + c
        first = pl.ds(pl.multiple_of(t * BLK, BLK), BLK)
        second = pl.ds(pl.multiple_of((slots * VB + t) * BLK, BLK), BLK)
        return (
            pltpu.make_async_copy(pk.at[rows, cols], out.at[first, :], sem.at[0, t]),
            pltpu.make_async_copy(pv.at[rows, cols], out.at[second, :], sem.at[1, t]),
        )

    def sinks():
        base = 2 * slots * VB * BLK
        return [
            pltpu.make_async_copy(
                ref.at[pl.ds(0, SINK), pl.ds(g * D, D)],
                out.at[pl.ds(base + (part * kv_count + g) * SINK, SINK), :],
                sink_sem.at[part, g],
            )
            for part, ref in enumerate((pk, pv))
            for g in range(kv_count)
        ]

    def each(act):
        def visit(head, rank):
            rank = jnp.where(lax.rem(head, SHARE) == 0, 0, rank)
            chosen = roles[head] == 1

            @pl.when(chosen)
            def _():
                slot = (head // SHARE) * MAX_RETRIEVERS + rank
                for c in range(VB):
                    col = columns[head, c]

                    @pl.when((c < col_count[head]) & (col // blocks_dev == seq[0]))
                    def _():
                        for copy in copies(head, slot, c, col):
                            act(copy)

            return rank + chosen.astype(jnp.int32)

        lax.fori_loop(0, kv_count * SHARE, visit, 0)

        @pl.when(seq[0] == 0)
        def _():
            for copy in sinks():
                act(copy)

    each(lambda copy: copy.start())
    each(lambda copy: copy.wait())


def collect(seq, roles, columns, col_count, prefix_keys, prefix_values, rows):
    kv_count = prefix_keys.shape[1] // D
    return pl.pallas_call(
        collect_kernel,
        grid_spec=pltpu.PrefetchScalarGridSpec(
            num_scalar_prefetch=4,
            grid=(1,),
            in_specs=[pl.BlockSpec(memory_space=pltpu.HBM)] * 2,
            out_specs=pl.BlockSpec((rows, D), lambda i, *_: (0, 0)),
            scratch_shapes=[
                pltpu.SemaphoreType.DMA((2, kv_count * MAX_RETRIEVERS * VB)),
                pltpu.SemaphoreType.DMA((2, kv_count)),
            ],
        ),
        out_shape=jax.ShapeDtypeStruct((rows, D), jnp.bfloat16),
        compiler_params=pltpu.CompilerParams(vmem_limit_bytes=VMEM_LIMIT),
        name="collect_columns",
    )(seq, roles, columns, col_count, prefix_keys, prefix_values)


def share_kernel(
    size,
    heads,
    orders,
    mine,
    queries,
    keys,
    values,
    cache_k,
    cache_v,
    out,
    q_out,
    kv_out,
    previous,
    acc,
    landed,
    send_sem,
    recv_sem,
    swap_send,
    swap_recv,
    tail_send,
    tail_recv,
    own_sem,
):
    me = lax.axis_index("seq")
    my_head = lax.axis_index("head")
    right, left = lax.rem(me + 1, size), lax.rem(me + size - 1, size)
    bits = len(orders[0])
    barrier = pltpu.get_barrier_semaphore()

    def bit_of(b):
        return lax.rem(me // (1 << b), 2)

    def partner(b):
        return me + (1 - 2 * bit_of(b)) * (1 << b)

    for b in range(bits):
        pl.semaphore_signal(
            barrier, inc=1, device_id={"seq": partner(b)}, device_id_type=pl.DeviceIdType.MESH
        )
    for d in range(1, heads):
        pl.semaphore_signal(
            barrier,
            inc=1,
            device_id={"head": lax.rem(my_head + d, heads)},
            device_id_type=pl.DeviceIdType.MESH,
        )
    for neighbour in (left, right):
        pl.semaphore_signal(
            barrier, inc=1, device_id={"seq": neighbour}, device_id_type=pl.DeviceIdType.MESH
        )
    pl.semaphore_wait(barrier, bits + heads + 1)

    rows_in, cache_width = keys.shape[0], cache_k.shape[1]
    my_rows = pl.ds(pl.multiple_of(my_head * rows_in, 16), rows_in)
    swaps = (
        (keys, kv_out.at[my_rows, pl.ds(0, cache_width)], cache_width),
        (values, kv_out.at[my_rows, pl.ds(cache_width, cache_width)], cache_width),
        (queries, q_out.at[my_rows, :], q_out.shape[1]),
    )
    swapped = []
    for n, (source, target, width) in enumerate(swaps):
        row = []
        for d in range(heads):
            to = lax.rem(my_head + d, heads)
            block = source.at[:, pl.ds(pl.multiple_of(to * width, D), width)]
            if d == 0:
                copy = pltpu.make_async_copy(block, target, own_sem.at[n])
            else:
                copy = pltpu.make_async_remote_copy(
                    src_ref=block,
                    dst_ref=target,
                    send_sem=swap_send.at[n, d - 1],
                    recv_sem=swap_recv.at[n, d - 1],
                    device_id={"head": to},
                    device_id_type=pl.DeviceIdType.MESH,
                )
            copy.start()
            row.append(copy)
        swapped.append(row)

    def tails(cached):
        copies = []
        for n, cache in enumerate((cache_k, cache_v)):
            place = pl.ds(n * cache_width, cache_width)
            if cached:
                source = cache.at[pl.ds(cache.shape[0] - WIN, WIN), :]
            else:
                source = kv_out.at[pl.ds(kv_out.shape[0] - WIN, WIN), place]
            copies.append(
                pltpu.make_async_remote_copy(
                    src_ref=source,
                    dst_ref=previous.at[:, place],
                    send_sem=tail_send.at[n],
                    recv_sem=tail_recv.at[n],
                    device_id={"seq": right},
                    device_id_type=pl.DeviceIdType.MESH,
                )
            )
        return copies

    def pass_tails():
        for row in swapped[:2]:
            for copy in row:
                copy.wait()

        @pl.when(me == size - 1)
        def _():
            for copy in tails(True):
                copy.start()

        @pl.when(me != size - 1)
        def _():
            for copy in tails(False):
                copy.start()

    streams = len(orders)
    part = mine.shape[0] // streams
    low = [part * w for w in range(streams)]
    length = [part] * streams
    started = {}

    def at(start, n):
        return pl.ds(pl.multiple_of(start, 16), n)

    def move(src, dst, w, step, b):
        copy = pltpu.make_async_remote_copy(
            src_ref=src,
            dst_ref=dst,
            send_sem=send_sem.at[w, step],
            recv_sem=recv_sem.at[w, step],
            device_id={"seq": partner(b)},
            device_id_type=pl.DeviceIdType.MESH,
        )
        copy.start()
        started[w, step] = copy

    def halve(w, step):
        b = orders[w][step]
        half = length[w] // 2
        source = mine if step == 0 else acc
        other = low[w] + (1 - bit_of(b)) * half
        place = part * w + part - length[w]
        move(source.at[at(other, half), :], landed.at[pl.ds(place, half), :], w, step, b)

    def add(w, step):
        b = orders[w][step]
        half = length[w] // 2
        source = mine if step == 0 else acc
        place = part * w + part - length[w]
        keep = at(low[w] + bit_of(b) * half, half)
        started[w, step].wait()
        into = out if step == bits - 1 else acc
        into[keep, :] = source[keep, :] + landed[pl.ds(place, half), :]
        low[w] = low[w] + bit_of(b) * half
        length[w] = half

    def double(w, step):
        b = orders[w][2 * bits - 1 - step]
        whole = out.at[at(low[w], length[w]), :]
        move(whole, whole, w, step, b)

    def join(w, step):
        b = orders[w][2 * bits - 1 - step]
        started[w, step].wait()
        low[w] = low[w] - bit_of(b) * length[w]
        length[w] = 2 * length[w]

    for step in range(2 * bits + 1):
        for w in range(streams):
            if 0 < step <= bits:
                add(w, step - 1)
            elif step > bits:
                join(w, step - 1)
            if step < bits:
                halve(w, step)
            elif step < 2 * bits:
                double(w, step)
        if step == 1:
            pass_tails()
    for copy in tails(False):
        copy.wait()
    for copy in swapped[2]:
        copy.wait()


def share(mine, queries, keys, values, prefix_keys, prefix_values):
    size, heads = lax.axis_size("seq"), lax.axis_size("head")
    bits = size.bit_length() - 1
    orders = [list(range(bits)), [0, *range(2, bits), 1]]
    rows = mine.shape[0]
    kind = mine.dtype
    span = keys.shape[0] * heads
    cache_width = prefix_keys.shape[1]
    anywhere = pl.BlockSpec(memory_space=pltpu.HBM)
    local = pl.BlockSpec(memory_space=pltpu.VMEM)
    return pl.pallas_call(
        functools.partial(share_kernel, size, heads, orders),
        out_shape=(
            jax.ShapeDtypeStruct(mine.shape, kind),
            jax.ShapeDtypeStruct((span, queries.shape[1] // heads), kind),
            jax.ShapeDtypeStruct((span, 2 * cache_width), kind),
            jax.ShapeDtypeStruct((WIN, 2 * cache_width), kind),
        ),
        in_specs=[local] + [anywhere] * 5,
        out_specs=(local, anywhere, anywhere, anywhere),
        scratch_shapes=[
            pltpu.VMEM((rows, D), kind),
            pltpu.VMEM((rows, D), kind),
            pltpu.SemaphoreType.DMA((len(orders), 2 * bits)),
            pltpu.SemaphoreType.DMA((len(orders), 2 * bits)),
            pltpu.SemaphoreType.DMA((3, heads - 1)),
            pltpu.SemaphoreType.DMA((3, heads - 1)),
            pltpu.SemaphoreType.DMA((2,)),
            pltpu.SemaphoreType.DMA((2,)),
            pltpu.SemaphoreType.DMA((3,)),
        ],
        compiler_params=pltpu.CompilerParams(
            collective_id=0, has_side_effects=True, vmem_limit_bytes=VMEM_LIMIT
        ),
        cost_estimate=pl.CostEstimate(
            flops=10**10, bytes_accessed=8 * rows * D, transcendentals=0
        ),
        name="share_columns",
    )(mine, queries, keys, values, prefix_keys, prefix_values)


def attend_kernel(
    roles,
    col_count,
    diagonals,
    q,
    k,
    v,
    pk,
    pv,
    sk,
    sv,
    far_k,
    far_v,
    out,
    keys_t,
    keys,
    vals,
    passers,
):
    group = pl.program_id(0)
    rows = q.shape[0]

    keys_t[:, :SINK] = sk[...].T
    keys_t[:, SINK : SINK + WIN] = pk[...].T
    keys_t[:, SINK + WIN :] = k[...].T
    keys[:WIN, :] = pk[...]
    keys[WIN:, :] = k[...]
    vals[:SINK, :D] = sv[...]
    vals[SINK : SINK + WIN, :D] = pv[...]
    vals[SINK + WIN :, :D] = v[...]
    vals[:, D:] = jnp.ones_like(vals[:, D:])

    def note(i, used):
        passes = roles[group * SHARE + i] != 1

        @pl.when(passes)
        def _():
            passers[used] = i
            passers[used + 1] = i

        return used + passes.astype(jnp.int32)

    used = lax.fori_loop(0, SHARE, note, 0)

    def lanes(i):
        return pl.ds(pl.multiple_of(i * D, D), D)

    def pass_pair(t, carry):
        pair = [lanes(passers[2 * t]), lanes(passers[2 * t + 1])]
        row = lax.rem(lax.broadcasted_iota(jnp.int32, (2 * QB, QB), 0), QB)
        col = lax.broadcasted_iota(jnp.int32, (2 * QB, QB), 1)
        for r in range(0, rows, QB):
            low, high = SINK + r, SINK + r + WIN + QB
            q_rows = jnp.concatenate([q[r : r + QB, place] for place in pair], 0)
            window = jnp.concatenate([keys_t[:, :SINK], keys_t[:, low:high]], 1)
            s = dot(q_rows, window)
            s = jnp.concatenate(
                [
                    s[:, :SINK],
                    jnp.where(col > row, s[:, SINK : SINK + QB], -jnp.inf),
                    s[:, SINK + QB : SINK + WIN],
                    jnp.where(col <= row, s[:, SINK + WIN :], -jnp.inf),
                ],
                1,
            )
            top = jnp.max(s, axis=1, keepdims=True)
            p = jnp.exp2((s - top) * SCALE).astype(jnp.bfloat16)
            acc = dot(p, jnp.concatenate([vals[:SINK, :], vals[low:high, :]], 0))
            done = (acc[:, :D] / acc[:, D:]).astype(out.dtype)
            for n, place in enumerate(pair):
                out[r : r + QB, place] = done[n * QB : (n + 1) * QB]
        return carry

    lax.fori_loop(0, (used + 1) // 2, pass_pair, 0)

    def retrieve(i, slot):
        head = group * SHARE + i
        chosen = roles[head] == 1

        @pl.when(chosen)
        def _():
            row = lax.broadcasted_iota(jnp.int32, (BLK, NSL * BLK), 0)
            col = lax.broadcasted_iota(jnp.int32, (BLK, NSL * BLK), 1)
            causal = (col <= row) | (col >= BLK)
            lane = lax.broadcasted_iota(jnp.int32, (1, VB * BLK), 1)
            open_cols = lane < col_count[head] * BLK
            place = pl.ds(pl.multiple_of(slot * (VB * BLK), VB * BLK), VB * BLK)
            vert_v = jnp.concatenate(
                [far_v[place, :], jnp.ones((VB * BLK, D), jnp.bfloat16)], 1
            )
            q_head = q[:, lanes(i)]
            s_vert = jnp.where(open_cols, dot_nt(q_head, far_k[place, :]), -jnp.inf)
            p_verts, slashes = [], []
            for r in range(0, rows, BLK):
                starts = [
                    pl.multiple_of(WIN + r - diagonals[head, t] * BLK, BLK) for t in range(NSL)
                ]
                near_k = jnp.concatenate([keys[pl.ds(at, BLK), :] for at in starts], 0)
                near_v = jnp.concatenate([vals[pl.ds(SINK + at, BLK), :] for at in starts], 0)
                s_near = jnp.where(causal, dot_nt(q_head[r : r + BLK], near_k), -jnp.inf)
                s_far = s_vert[r : r + BLK]
                top = jnp.maximum(
                    jnp.max(s_near, axis=1, keepdims=True), jnp.max(s_far, axis=1, keepdims=True)
                )
                p_near = jnp.exp2((s_near - top) * SCALE).astype(jnp.bfloat16)
                p_verts.append(jnp.exp2((s_far - top) * SCALE).astype(jnp.bfloat16))
                slashes.append(dot(p_near, near_v))
            acc = dot(jnp.concatenate(p_verts, 0), vert_v) + jnp.concatenate(slashes, 0)
            out[:, lanes(i)] = (acc[:, :D] / acc[:, D:]).astype(out.dtype)

        return slot + chosen.astype(jnp.int32)

    lax.fori_loop(0, SHARE, retrieve, 0)


def attend(roles, col_count, diagonals, q, kv, previous, shared):
    rows, width = q.shape
    kv_count = kv.shape[1] // (2 * D)
    far_rows = MAX_RETRIEVERS * VB * BLK
    sink_block = 2 * kv_count * far_rows // SINK

    def whole(g, *_):
        return (0, g)

    def value(g, *_):
        return (0, kv_count + g)

    return pl.pallas_call(
        attend_kernel,
        grid_spec=pltpu.PrefetchScalarGridSpec(
            num_scalar_prefetch=3,
            grid=(kv_count,),
            in_specs=[
                pl.BlockSpec((rows, SHARE * D), whole),
                pl.BlockSpec((rows, D), whole),
                pl.BlockSpec((rows, D), value),
                pl.BlockSpec((WIN, D), whole),
                pl.BlockSpec((WIN, D), value),
                pl.BlockSpec((SINK, D), lambda g, *_: (sink_block + g, 0)),
                pl.BlockSpec((SINK, D), lambda g, *_: (sink_block + kv_count + g, 0)),
                pl.BlockSpec((far_rows, D), lambda g, *_: (g, 0)),
                pl.BlockSpec((far_rows, D), lambda g, *_: (kv_count + g, 0)),
            ],
            out_specs=pl.BlockSpec((rows, SHARE * D), whole),
            scratch_shapes=[
                pltpu.VMEM((D, SINK + WIN + rows), jnp.bfloat16),
                pltpu.VMEM((WIN + rows, D), jnp.bfloat16),
                pltpu.VMEM((SINK + WIN + rows, 2 * D), jnp.bfloat16),
                pltpu.SMEM((2 * SHARE,), jnp.int32),
            ],
        ),
        out_shape=jax.ShapeDtypeStruct((rows, width), jnp.bfloat16),
        compiler_params=pltpu.CompilerParams(vmem_limit_bytes=VMEM_LIMIT),
        cost_estimate=pl.CostEstimate(
            flops=8 * width * rows * (SINK + WIN + QB),
            bytes_accessed=4 * rows * width,
            transcendentals=width // D * rows * (SINK + WIN + QB),
        ),
        name="attend",
    )(roles, col_count, diagonals, q, kv, kv, previous, previous, shared, shared, shared, shared)


def shards(queries, keys, values, prefix_keys, prefix_values, roles, columns, col_count, diagonals):
    seq_size = lax.axis_size("seq")
    seq = lax.axis_index("seq").astype(jnp.int32).reshape(1)
    kv_count = prefix_keys.shape[1] // D
    needed = 2 * kv_count * (MAX_RETRIEVERS * VB * BLK + SINK)
    unit = 2 * 16 * seq_size
    rows = -(-needed // unit) * unit
    mine = collect(seq, roles, columns, col_count, prefix_keys, prefix_values, rows)
    shared, q, kv, previous = share(mine, queries, keys, values, prefix_keys, prefix_values)
    return attend(roles, col_count, diagonals, q, kv, previous, shared)


def solution(mesh):
    placed = (
        P(("seq", "head"), None),
        P(("seq", "head"), None),
        P(("seq", "head"), None),
        P("seq", "head"),
        P("seq", "head"),
        P("head"),
        P("head", None),
        P("head"),
        P("head", None),
    )
    return jax.shard_map(
        shards, mesh=mesh, in_specs=placed, out_specs=P("seq", "head"), check_vma=False
    )
```

```python
import functools
import math

import jax
import jax.numpy as jnp
from jax import lax
from jax.experimental import pallas as pl
from jax.experimental.pallas import tpu as pltpu
from jax.sharding import PartitionSpec as P

QUERY_HEADS = 64
KEY_VALUE_HEADS = 8
SHARE = QUERY_HEADS // KEY_VALUE_HEADS
D = 128
SINK = 128
WIN = 512
BLK = 64
VB = 6
NSL = 4
MAX_RETRIEVERS = 4
QB = 128
STREAMS = 4
SCALE = math.log2(math.e) / math.sqrt(D)
VMEM_LIMIT = 58 * 1024 * 1024


def dot_nt(a, b):
    return lax.dot_general(a, b, (((1,), (1,)), ((), ())), preferred_element_type=jnp.float32)


def dot(a, b):
    return jnp.dot(a, b, preferred_element_type=jnp.float32)


def collect_kernel(seq, roles, columns, col_count, pk, pv, out, sem, sink_sem):
    blocks_dev = pk.shape[0] // BLK
    kv_count = pk.shape[1] // D
    slots = kv_count * MAX_RETRIEVERS
    out[...] = jnp.zeros_like(out)

    def copies(head, slot, c, col):
        local = col - seq[0] * blocks_dev
        rows = pl.ds(pl.multiple_of(local * BLK, BLK), BLK)
        cols = pl.ds(pl.multiple_of((head // SHARE) * D, D), D)
        t = slot * VB + c
        first = pl.ds(pl.multiple_of(t * BLK, BLK), BLK)
        second = pl.ds(pl.multiple_of((slots * VB + t) * BLK, BLK), BLK)
        return (
            pltpu.make_async_copy(pk.at[rows, cols], out.at[first, :], sem.at[0, t]),
            pltpu.make_async_copy(pv.at[rows, cols], out.at[second, :], sem.at[1, t]),
        )

    def sinks():
        base = 2 * slots * VB * BLK
        return [
            pltpu.make_async_copy(
                ref.at[pl.ds(0, SINK), pl.ds(g * D, D)],
                out.at[pl.ds(base + (part * kv_count + g) * SINK, SINK), :],
                sink_sem.at[part, g],
            )
            for part, ref in enumerate((pk, pv))
            for g in range(kv_count)
        ]

    def each(act):
        def visit(head, rank):
            rank = jnp.where(lax.rem(head, SHARE) == 0, 0, rank)
            chosen = roles[head] == 1

            @pl.when(chosen)
            def _():
                slot = (head // SHARE) * MAX_RETRIEVERS + rank
                for c in range(VB):
                    col = columns[head, c]

                    @pl.when((c < col_count[head]) & (col // blocks_dev == seq[0]))
                    def _():
                        for copy in copies(head, slot, c, col):
                            act(copy)

            return rank + chosen.astype(jnp.int32)

        lax.fori_loop(0, kv_count * SHARE, visit, 0)

        @pl.when(seq[0] == 0)
        def _():
            for copy in sinks():
                act(copy)

    each(lambda copy: copy.start())
    each(lambda copy: copy.wait())


def collect(seq, roles, columns, col_count, prefix_keys, prefix_values, rows):
    kv_count = prefix_keys.shape[1] // D
    return pl.pallas_call(
        collect_kernel,
        grid_spec=pltpu.PrefetchScalarGridSpec(
            num_scalar_prefetch=4,
            grid=(1,),
            in_specs=[pl.BlockSpec(memory_space=pltpu.HBM)] * 2,
            out_specs=pl.BlockSpec((rows, D), lambda i, *_: (0, 0)),
            scratch_shapes=[
                pltpu.SemaphoreType.DMA((2, kv_count * MAX_RETRIEVERS * VB)),
                pltpu.SemaphoreType.DMA((2, kv_count)),
            ],
        ),
        out_shape=jax.ShapeDtypeStruct((rows, D), jnp.bfloat16),
        compiler_params=pltpu.CompilerParams(vmem_limit_bytes=VMEM_LIMIT),
        name="collect_columns",
    )(seq, roles, columns, col_count, prefix_keys, prefix_values)


def share_kernel(
    size,
    heads,
    orders,
    mine,
    queries,
    keys,
    values,
    cache_k,
    cache_v,
    out,
    q_out,
    kv_out,
    previous,
    acc,
    landed,
    send_sem,
    recv_sem,
    swap_send,
    swap_recv,
    tail_send,
    tail_recv,
    own_sem,
):
    me = lax.axis_index("seq")
    my_head = lax.axis_index("head")
    right, left = lax.rem(me + 1, size), lax.rem(me + size - 1, size)
    bits = len(orders[0])
    barrier = pltpu.get_barrier_semaphore()

    def bit_of(b):
        return lax.rem(me // (1 << b), 2)

    def partner(b):
        return me + (1 - 2 * bit_of(b)) * (1 << b)

    for b in range(bits):
        pl.semaphore_signal(
            barrier, inc=1, device_id={"seq": partner(b)}, device_id_type=pl.DeviceIdType.MESH
        )
    for d in range(1, heads):
        pl.semaphore_signal(
            barrier,
            inc=1,
            device_id={"head": lax.rem(my_head + d, heads)},
            device_id_type=pl.DeviceIdType.MESH,
        )
    for neighbour in (left, right):
        pl.semaphore_signal(
            barrier, inc=1, device_id={"seq": neighbour}, device_id_type=pl.DeviceIdType.MESH
        )
    pl.semaphore_wait(barrier, bits + heads + 1)

    rows_in, cache_width = keys.shape[0], cache_k.shape[1]
    my_rows = pl.ds(pl.multiple_of(my_head * rows_in, 16), rows_in)
    swaps = (
        (keys, kv_out.at[my_rows, pl.ds(0, cache_width)], cache_width),
        (values, kv_out.at[my_rows, pl.ds(cache_width, cache_width)], cache_width),
        (queries, q_out.at[my_rows, :], q_out.shape[1]),
    )
    swapped = []
    for n, (source, target, width) in enumerate(swaps):
        row = []
        for d in range(heads):
            to = lax.rem(my_head + d, heads)
            block = source.at[:, pl.ds(pl.multiple_of(to * width, D), width)]
            if d == 0:
                copy = pltpu.make_async_copy(block, target, own_sem.at[n])
            else:
                copy = pltpu.make_async_remote_copy(
                    src_ref=block,
                    dst_ref=target,
                    send_sem=swap_send.at[n, d - 1],
                    recv_sem=swap_recv.at[n, d - 1],
                    device_id={"head": to},
                    device_id_type=pl.DeviceIdType.MESH,
                )
            copy.start()
            row.append(copy)
        swapped.append(row)

    def tails(cached):
        copies = []
        for n, cache in enumerate((cache_k, cache_v)):
            place = pl.ds(n * cache_width, cache_width)
            if cached:
                source = cache.at[pl.ds(cache.shape[0] - WIN, WIN), :]
            else:
                source = kv_out.at[pl.ds(kv_out.shape[0] - WIN, WIN), place]
            copies.append(
                pltpu.make_async_remote_copy(
                    src_ref=source,
                    dst_ref=previous.at[:, place],
                    send_sem=tail_send.at[n],
                    recv_sem=tail_recv.at[n],
                    device_id={"seq": right},
                    device_id_type=pl.DeviceIdType.MESH,
                )
            )
        return copies

    def pass_tails():
        for row in swapped[:2]:
            for copy in row:
                copy.wait()

        @pl.when(me == size - 1)
        def _():
            for copy in tails(True):
                copy.start()

        @pl.when(me != size - 1)
        def _():
            for copy in tails(False):
                copy.start()

    streams = len(orders)
    part = mine.shape[0] // streams
    low = [part * w for w in range(streams)]
    length = [part] * streams
    started = {}

    def at(start, n):
        return pl.ds(pl.multiple_of(start, 16), n)

    def move(src, dst, w, step, b):
        copy = pltpu.make_async_remote_copy(
            src_ref=src,
            dst_ref=dst,
            send_sem=send_sem.at[w, step],
            recv_sem=recv_sem.at[w, step],
            device_id={"seq": partner(b)},
            device_id_type=pl.DeviceIdType.MESH,
        )
        copy.start()
        started[w, step] = copy

    def halve(w, step):
        b = orders[w][step]
        half = length[w] // 2
        source = mine if step == 0 else acc
        other = low[w] + (1 - bit_of(b)) * half
        place = part * w + part - length[w]
        move(source.at[at(other, half), :], landed.at[pl.ds(place, half), :], w, step, b)

    def add(w, step):
        b = orders[w][step]
        half = length[w] // 2
        source = mine if step == 0 else acc
        place = part * w + part - length[w]
        keep = at(low[w] + bit_of(b) * half, half)
        started[w, step].wait()
        into = out if step == bits - 1 else acc
        into[keep, :] = source[keep, :] + landed[pl.ds(place, half), :]
        low[w] = low[w] + bit_of(b) * half
        length[w] = half

    def double(w, step):
        b = orders[w][2 * bits - 1 - step]
        whole = out.at[at(low[w], length[w]), :]
        move(whole, whole, w, step, b)

    def join(w, step):
        b = orders[w][2 * bits - 1 - step]
        started[w, step].wait()
        low[w] = low[w] - bit_of(b) * length[w]
        length[w] = 2 * length[w]

    for step in range(2 * bits + 1):
        for w in range(streams):
            if 0 < step <= bits:
                add(w, step - 1)
            elif step > bits:
                join(w, step - 1)
            if step < bits:
                halve(w, step)
            elif step < 2 * bits:
                double(w, step)
        if step == 1:
            pass_tails()
    for copy in tails(False):
        copy.wait()
    for copy in swapped[2]:
        copy.wait()


def share(mine, queries, keys, values, prefix_keys, prefix_values):
    size, heads = lax.axis_size("seq"), lax.axis_size("head")
    bits = size.bit_length() - 1
    orders = [list(range(bits)), [0, *range(2, bits), 1]] * (STREAMS // 2)
    rows = mine.shape[0]
    kind = mine.dtype
    span = keys.shape[0] * heads
    cache_width = prefix_keys.shape[1]
    anywhere = pl.BlockSpec(memory_space=pltpu.HBM)
    local = pl.BlockSpec(memory_space=pltpu.VMEM)
    return pl.pallas_call(
        functools.partial(share_kernel, size, heads, orders),
        out_shape=(
            jax.ShapeDtypeStruct(mine.shape, kind),
            jax.ShapeDtypeStruct((span, queries.shape[1] // heads), kind),
            jax.ShapeDtypeStruct((span, 2 * cache_width), kind),
            jax.ShapeDtypeStruct((WIN, 2 * cache_width), kind),
        ),
        in_specs=[local] + [anywhere] * 5,
        out_specs=(local, anywhere, anywhere, anywhere),
        scratch_shapes=[
            pltpu.VMEM((rows, D), kind),
            pltpu.VMEM((rows, D), kind),
            pltpu.SemaphoreType.DMA((len(orders), 2 * bits)),
            pltpu.SemaphoreType.DMA((len(orders), 2 * bits)),
            pltpu.SemaphoreType.DMA((3, heads - 1)),
            pltpu.SemaphoreType.DMA((3, heads - 1)),
            pltpu.SemaphoreType.DMA((2,)),
            pltpu.SemaphoreType.DMA((2,)),
            pltpu.SemaphoreType.DMA((3,)),
        ],
        compiler_params=pltpu.CompilerParams(
            collective_id=0, has_side_effects=True, vmem_limit_bytes=VMEM_LIMIT
        ),
        cost_estimate=pl.CostEstimate(
            flops=10**10, bytes_accessed=8 * rows * D, transcendentals=0
        ),
        name="share_columns",
    )(mine, queries, keys, values, prefix_keys, prefix_values)


def attend_kernel(
    roles,
    col_count,
    diagonals,
    q,
    k,
    v,
    pk,
    pv,
    sk,
    sv,
    far_k,
    far_v,
    out,
    keys_t,
    keys,
    vals,
    passers,
):
    group = pl.program_id(0)
    rows = q.shape[0]

    keys_t[:, :SINK] = sk[...].T
    keys_t[:, SINK : SINK + WIN] = pk[...].T
    keys_t[:, SINK + WIN :] = k[...].T
    keys[:WIN, :] = pk[...]
    keys[WIN:, :] = k[...]
    vals[:SINK, :D] = sv[...]
    vals[SINK : SINK + WIN, :D] = pv[...]
    vals[SINK + WIN :, :D] = v[...]
    vals[:, D:] = jnp.ones_like(vals[:, D:])

    def note(i, used):
        passes = roles[group * SHARE + i] != 1

        @pl.when(passes)
        def _():
            passers[used] = i
            passers[used + 1] = i

        return used + passes.astype(jnp.int32)

    used = lax.fori_loop(0, SHARE, note, 0)

    def lanes(i):
        return pl.ds(pl.multiple_of(i * D, D), D)

    def pass_pair(t, carry):
        pair = [lanes(passers[2 * t]), lanes(passers[2 * t + 1])]
        row = lax.rem(lax.broadcasted_iota(jnp.int32, (2 * QB, QB), 0), QB)
        col = lax.broadcasted_iota(jnp.int32, (2 * QB, QB), 1)
        for r in range(0, rows, QB):
            low, high = SINK + r, SINK + r + WIN + QB
            q_rows = jnp.concatenate([q[r : r + QB, place] for place in pair], 0)
            window = jnp.concatenate([keys_t[:, :SINK], keys_t[:, low:high]], 1)
            s = dot(q_rows, window)
            s = jnp.concatenate(
                [
                    s[:, :SINK],
                    jnp.where(col > row, s[:, SINK : SINK + QB], -jnp.inf),
                    s[:, SINK + QB : SINK + WIN],
                    jnp.where(col <= row, s[:, SINK + WIN :], -jnp.inf),
                ],
                1,
            )
            top = jnp.max(s, axis=1, keepdims=True)
            p = jnp.exp2((s - top) * SCALE).astype(jnp.bfloat16)
            acc = dot(p, jnp.concatenate([vals[:SINK, :], vals[low:high, :]], 0))
            done = (acc[:, :D] / acc[:, D:]).astype(out.dtype)
            for n, place in enumerate(pair):
                out[r : r + QB, place] = done[n * QB : (n + 1) * QB]
        return carry

    lax.fori_loop(0, (used + 1) // 2, pass_pair, 0)

    def retrieve(i, slot):
        head = group * SHARE + i
        chosen = roles[head] == 1

        @pl.when(chosen)
        def _():
            row = lax.broadcasted_iota(jnp.int32, (BLK, NSL * BLK), 0)
            col = lax.broadcasted_iota(jnp.int32, (BLK, NSL * BLK), 1)
            causal = (col <= row) | (col >= BLK)
            lane = lax.broadcasted_iota(jnp.int32, (1, VB * BLK), 1)
            open_cols = lane < col_count[head] * BLK
            place = pl.ds(pl.multiple_of(slot * (VB * BLK), VB * BLK), VB * BLK)
            vert_v = jnp.concatenate(
                [far_v[place, :], jnp.ones((VB * BLK, D), jnp.bfloat16)], 1
            )
            q_head = q[:, lanes(i)]
            s_vert = jnp.where(open_cols, dot_nt(q_head, far_k[place, :]), -jnp.inf)
            p_verts, slashes = [], []
            for r in range(0, rows, BLK):
                starts = [
                    pl.multiple_of(WIN + r - diagonals[head, t] * BLK, BLK) for t in range(NSL)
                ]
                near_k = jnp.concatenate([keys[pl.ds(at, BLK), :] for at in starts], 0)
                near_v = jnp.concatenate([vals[pl.ds(SINK + at, BLK), :] for at in starts], 0)
                s_near = jnp.where(causal, dot_nt(q_head[r : r + BLK], near_k), -jnp.inf)
                s_far = s_vert[r : r + BLK]
                top = jnp.maximum(
                    jnp.max(s_near, axis=1, keepdims=True), jnp.max(s_far, axis=1, keepdims=True)
                )
                p_near = jnp.exp2((s_near - top) * SCALE).astype(jnp.bfloat16)
                p_verts.append(jnp.exp2((s_far - top) * SCALE).astype(jnp.bfloat16))
                slashes.append(dot(p_near, near_v))
            acc = dot(jnp.concatenate(p_verts, 0), vert_v) + jnp.concatenate(slashes, 0)
            out[:, lanes(i)] = (acc[:, :D] / acc[:, D:]).astype(out.dtype)

        return slot + chosen.astype(jnp.int32)

    lax.fori_loop(0, SHARE, retrieve, 0)


def attend(roles, col_count, diagonals, q, kv, previous, shared):
    rows, width = q.shape
    kv_count = kv.shape[1] // (2 * D)
    far_rows = MAX_RETRIEVERS * VB * BLK
    sink_block = 2 * kv_count * far_rows // SINK

    def whole(g, *_):
        return (0, g)

    def value(g, *_):
        return (0, kv_count + g)

    return pl.pallas_call(
        attend_kernel,
        grid_spec=pltpu.PrefetchScalarGridSpec(
            num_scalar_prefetch=3,
            grid=(kv_count,),
            in_specs=[
                pl.BlockSpec((rows, SHARE * D), whole),
                pl.BlockSpec((rows, D), whole),
                pl.BlockSpec((rows, D), value),
                pl.BlockSpec((WIN, D), whole),
                pl.BlockSpec((WIN, D), value),
                pl.BlockSpec((SINK, D), lambda g, *_: (sink_block + g, 0)),
                pl.BlockSpec((SINK, D), lambda g, *_: (sink_block + kv_count + g, 0)),
                pl.BlockSpec((far_rows, D), lambda g, *_: (g, 0)),
                pl.BlockSpec((far_rows, D), lambda g, *_: (kv_count + g, 0)),
            ],
            out_specs=pl.BlockSpec((rows, SHARE * D), whole),
            scratch_shapes=[
                pltpu.VMEM((D, SINK + WIN + rows), jnp.bfloat16),
                pltpu.VMEM((WIN + rows, D), jnp.bfloat16),
                pltpu.VMEM((SINK + WIN + rows, 2 * D), jnp.bfloat16),
                pltpu.SMEM((2 * SHARE,), jnp.int32),
            ],
        ),
        out_shape=jax.ShapeDtypeStruct((rows, width), jnp.bfloat16),
        compiler_params=pltpu.CompilerParams(vmem_limit_bytes=VMEM_LIMIT),
        cost_estimate=pl.CostEstimate(
            flops=8 * width * rows * (SINK + WIN + QB),
            bytes_accessed=4 * rows * width,
            transcendentals=width // D * rows * (SINK + WIN + QB),
        ),
        name="attend",
    )(roles, col_count, diagonals, q, kv, kv, previous, previous, shared, shared, shared, shared)


def shards(queries, keys, values, prefix_keys, prefix_values, roles, columns, col_count, diagonals):
    seq_size = lax.axis_size("seq")
    seq = lax.axis_index("seq").astype(jnp.int32).reshape(1)
    kv_count = prefix_keys.shape[1] // D
    needed = 2 * kv_count * (MAX_RETRIEVERS * VB * BLK + SINK)
    unit = STREAMS * 16 * seq_size
    rows = -(-needed // unit) * unit
    mine = collect(seq, roles, columns, col_count, prefix_keys, prefix_values, rows)
    shared, q, kv, previous = share(mine, queries, keys, values, prefix_keys, prefix_values)
    return attend(roles, col_count, diagonals, q, kv, previous, shared)


def solution(mesh):
    placed = (
        P(("seq", "head"), None),
        P(("seq", "head"), None),
        P(("seq", "head"), None),
        P("seq", "head"),
        P("seq", "head"),
        P("head"),
        P("head", None),
        P("head"),
        P("head", None),
    )
    return jax.shard_map(
        shards, mesh=mesh, in_specs=placed, out_specs=P("seq", "head"), check_vma=False
    )
```

```python
import functools
import math

import jax
import jax.numpy as jnp
from jax import lax
from jax.experimental import pallas as pl
from jax.experimental.pallas import tpu as pltpu
from jax.sharding import PartitionSpec as P

QUERY_HEADS = 64
KEY_VALUE_HEADS = 8
SHARE = QUERY_HEADS // KEY_VALUE_HEADS
D = 128
SINK = 128
WIN = 512
BLK = 64
VB = 6
NSL = 4
MAX_RETRIEVERS = 4
QB = 128
SCALE = math.log2(math.e) / math.sqrt(D)
VMEM_LIMIT = 40 * 1024 * 1024


def dot_nt(a, b):
    return lax.dot_general(a, b, (((1,), (1,)), ((), ())), preferred_element_type=jnp.float32)


def dot(a, b):
    return jnp.dot(a, b, preferred_element_type=jnp.float32)


def collect_kernel(seq, roles, columns, col_count, pk, pv, out, sem, sink_sem):
    blocks_dev = pk.shape[0] // BLK
    kv_count = pk.shape[1] // D
    slots = kv_count * MAX_RETRIEVERS
    out[...] = jnp.zeros_like(out)

    def copies(head, slot, c, col):
        local = col - seq[0] * blocks_dev
        rows = pl.ds(pl.multiple_of(local * BLK, BLK), BLK)
        cols = pl.ds(pl.multiple_of((head // SHARE) * D, D), D)
        t = slot * VB + c
        first = pl.ds(pl.multiple_of(t * BLK, BLK), BLK)
        second = pl.ds(pl.multiple_of((slots * VB + t) * BLK, BLK), BLK)
        return (
            pltpu.make_async_copy(pk.at[rows, cols], out.at[first, :], sem.at[0, t]),
            pltpu.make_async_copy(pv.at[rows, cols], out.at[second, :], sem.at[1, t]),
        )

    def sinks():
        base = 2 * slots * VB * BLK
        return [
            pltpu.make_async_copy(
                ref.at[pl.ds(0, SINK), pl.ds(g * D, D)],
                out.at[pl.ds(base + (part * kv_count + g) * SINK, SINK), :],
                sink_sem.at[part, g],
            )
            for part, ref in enumerate((pk, pv))
            for g in range(kv_count)
        ]

    def each(act):
        def visit(head, rank):
            rank = jnp.where(lax.rem(head, SHARE) == 0, 0, rank)
            chosen = roles[head] == 1

            @pl.when(chosen)
            def _():
                slot = (head // SHARE) * MAX_RETRIEVERS + rank
                for c in range(VB):
                    col = columns[head, c]

                    @pl.when((c < col_count[head]) & (col // blocks_dev == seq[0]))
                    def _():
                        for copy in copies(head, slot, c, col):
                            act(copy)

            return rank + chosen.astype(jnp.int32)

        lax.fori_loop(0, kv_count * SHARE, visit, 0)

        @pl.when(seq[0] == 0)
        def _():
            for copy in sinks():
                act(copy)

    each(lambda copy: copy.start())
    each(lambda copy: copy.wait())


def collect(seq, roles, columns, col_count, prefix_keys, prefix_values, rows):
    kv_count = prefix_keys.shape[1] // D
    return pl.pallas_call(
        collect_kernel,
        grid_spec=pltpu.PrefetchScalarGridSpec(
            num_scalar_prefetch=4,
            grid=(1,),
            in_specs=[pl.BlockSpec(memory_space=pltpu.HBM)] * 2,
            out_specs=pl.BlockSpec((rows, D), lambda i, *_: (0, 0)),
            scratch_shapes=[
                pltpu.SemaphoreType.DMA((2, kv_count * MAX_RETRIEVERS * VB)),
                pltpu.SemaphoreType.DMA((2, kv_count)),
            ],
        ),
        out_shape=jax.ShapeDtypeStruct((rows, D), jnp.bfloat16),
        compiler_params=pltpu.CompilerParams(vmem_limit_bytes=VMEM_LIMIT),
        name="collect_columns",
    )(seq, roles, columns, col_count, prefix_keys, prefix_values)


def share_kernel(
    size,
    heads,
    orders,
    mine,
    queries,
    keys,
    values,
    cache_k,
    cache_v,
    out,
    q_out,
    kv_out,
    previous,
    acc,
    landed,
    send_sem,
    recv_sem,
    swap_send,
    swap_recv,
    tail_send,
    tail_recv,
    own_sem,
):
    me = lax.axis_index("seq")
    my_head = lax.axis_index("head")
    right, left = lax.rem(me + 1, size), lax.rem(me + size - 1, size)
    bits = len(orders[0])
    barrier = pltpu.get_barrier_semaphore()

    def bit_of(b):
        return lax.rem(me // (1 << b), 2)

    def partner(b):
        return me + (1 - 2 * bit_of(b)) * (1 << b)

    for b in range(bits):
        pl.semaphore_signal(
            barrier, inc=1, device_id={"seq": partner(b)}, device_id_type=pl.DeviceIdType.MESH
        )
    for d in range(1, heads):
        pl.semaphore_signal(
            barrier,
            inc=1,
            device_id={"head": lax.rem(my_head + d, heads)},
            device_id_type=pl.DeviceIdType.MESH,
        )
    for neighbour in (left, right):
        pl.semaphore_signal(
            barrier, inc=1, device_id={"seq": neighbour}, device_id_type=pl.DeviceIdType.MESH
        )
    pl.semaphore_wait(barrier, bits + heads + 1)

    rows_in, cache_width = keys.shape[0], cache_k.shape[1]
    my_rows = pl.ds(pl.multiple_of(my_head * rows_in, 16), rows_in)
    swaps = (
        (keys, kv_out.at[my_rows, pl.ds(0, cache_width)], cache_width),
        (values, kv_out.at[my_rows, pl.ds(cache_width, cache_width)], cache_width),
        (queries, q_out.at[my_rows, :], q_out.shape[1]),
    )
    swapped = []
    for n, (source, target, width) in enumerate(swaps):
        row = []
        for d in range(heads):
            to = lax.rem(my_head + d, heads)
            block = source.at[:, pl.ds(pl.multiple_of(to * width, D), width)]
            if d == 0:
                copy = pltpu.make_async_copy(block, target, own_sem.at[n])
            else:
                copy = pltpu.make_async_remote_copy(
                    src_ref=block,
                    dst_ref=target,
                    send_sem=swap_send.at[n, d - 1],
                    recv_sem=swap_recv.at[n, d - 1],
                    device_id={"head": to},
                    device_id_type=pl.DeviceIdType.MESH,
                )
            copy.start()
            row.append(copy)
        swapped.append(row)

    def tails(cached):
        copies = []
        for n, cache in enumerate((cache_k, cache_v)):
            place = pl.ds(n * cache_width, cache_width)
            if cached:
                source = cache.at[pl.ds(cache.shape[0] - WIN, WIN), :]
            else:
                source = kv_out.at[pl.ds(kv_out.shape[0] - WIN, WIN), place]
            copies.append(
                pltpu.make_async_remote_copy(
                    src_ref=source,
                    dst_ref=previous.at[:, place],
                    send_sem=tail_send.at[n],
                    recv_sem=tail_recv.at[n],
                    device_id={"seq": right},
                    device_id_type=pl.DeviceIdType.MESH,
                )
            )
        return copies

    def pass_tails():
        for row in swapped[:2]:
            for copy in row:
                copy.wait()

        @pl.when(me == size - 1)
        def _():
            for copy in tails(True):
                copy.start()

        @pl.when(me != size - 1)
        def _():
            for copy in tails(False):
                copy.start()

    streams = len(orders)
    part = mine.shape[0] // streams
    low = [part * w for w in range(streams)]
    length = [part] * streams
    started = {}

    def at(start, n):
        return pl.ds(pl.multiple_of(start, 16), n)

    def move(src, dst, w, step, b):
        copy = pltpu.make_async_remote_copy(
            src_ref=src,
            dst_ref=dst,
            send_sem=send_sem.at[w, step],
            recv_sem=recv_sem.at[w, step],
            device_id={"seq": partner(b)},
            device_id_type=pl.DeviceIdType.MESH,
        )
        copy.start()
        started[w, step] = copy

    def halve(w, step):
        b = orders[w][step]
        half = length[w] // 2
        source = mine if step == 0 else acc
        other = low[w] + (1 - bit_of(b)) * half
        place = part * w + part - length[w]
        move(source.at[at(other, half), :], landed.at[pl.ds(place, half), :], w, step, b)

    def add(w, step):
        b = orders[w][step]
        half = length[w] // 2
        source = mine if step == 0 else acc
        place = part * w + part - length[w]
        keep = at(low[w] + bit_of(b) * half, half)
        started[w, step].wait()
        into = out if step == bits - 1 else acc
        into[keep, :] = source[keep, :] + landed[pl.ds(place, half), :]
        low[w] = low[w] + bit_of(b) * half
        length[w] = half

    def double(w, step):
        b = orders[w][2 * bits - 1 - step]
        whole = out.at[at(low[w], length[w]), :]
        move(whole, whole, w, step, b)

    def join(w, step):
        b = orders[w][2 * bits - 1 - step]
        started[w, step].wait()
        low[w] = low[w] - bit_of(b) * length[w]
        length[w] = 2 * length[w]

    for step in range(2 * bits + 1):
        for w in range(streams):
            if 0 < step <= bits:
                add(w, step - 1)
            elif step > bits:
                join(w, step - 1)
            if step < bits:
                halve(w, step)
            elif step < 2 * bits:
                double(w, step)
        if step == bits - 1:
            pass_tails()
    for copy in tails(False):
        copy.wait()
    for copy in swapped[2]:
        copy.wait()


def share(mine, queries, keys, values, prefix_keys, prefix_values):
    size, heads = lax.axis_size("seq"), lax.axis_size("head")
    bits = size.bit_length() - 1
    orders = [list(range(bits)), [0, 2, 1, *range(3, bits)]]
    rows = mine.shape[0]
    kind = mine.dtype
    span = keys.shape[0] * heads
    cache_width = prefix_keys.shape[1]
    anywhere = pl.BlockSpec(memory_space=pltpu.HBM)
    local = pl.BlockSpec(memory_space=pltpu.VMEM)
    return pl.pallas_call(
        functools.partial(share_kernel, size, heads, orders),
        out_shape=(
            jax.ShapeDtypeStruct(mine.shape, kind),
            jax.ShapeDtypeStruct((span, queries.shape[1] // heads), kind),
            jax.ShapeDtypeStruct((span, 2 * cache_width), kind),
            jax.ShapeDtypeStruct((WIN, 2 * cache_width), kind),
        ),
        in_specs=[local] + [anywhere] * 5,
        out_specs=(local, anywhere, anywhere, anywhere),
        scratch_shapes=[
            pltpu.VMEM((rows, D), kind),
            pltpu.VMEM((rows, D), kind),
            pltpu.SemaphoreType.DMA((len(orders), 2 * bits)),
            pltpu.SemaphoreType.DMA((len(orders), 2 * bits)),
            pltpu.SemaphoreType.DMA((3, heads - 1)),
            pltpu.SemaphoreType.DMA((3, heads - 1)),
            pltpu.SemaphoreType.DMA((2,)),
            pltpu.SemaphoreType.DMA((2,)),
            pltpu.SemaphoreType.DMA((3,)),
        ],
        compiler_params=pltpu.CompilerParams(
            collective_id=0, has_side_effects=True, vmem_limit_bytes=VMEM_LIMIT
        ),
        cost_estimate=pl.CostEstimate(
            flops=10**10, bytes_accessed=8 * rows * D, transcendentals=0
        ),
        name="share_columns",
    )(mine, queries, keys, values, prefix_keys, prefix_values)


def attend_kernel(
    roles,
    col_count,
    diagonals,
    q,
    k,
    v,
    pk,
    pv,
    sk,
    sv,
    far_k,
    far_v,
    out,
    keys_t,
    keys,
    vals,
    passers,
):
    group = pl.program_id(0)
    rows = q.shape[0]

    keys_t[:, :SINK] = sk[...].T
    keys_t[:, SINK : SINK + WIN] = pk[...].T
    keys_t[:, SINK + WIN :] = k[...].T
    keys[:WIN, :] = pk[...]
    keys[WIN:, :] = k[...]
    vals[:SINK, :D] = sv[...]
    vals[SINK : SINK + WIN, :D] = pv[...]
    vals[SINK + WIN :, :D] = v[...]
    vals[:, D:] = jnp.ones_like(vals[:, D:])

    def note(i, used):
        passes = roles[group * SHARE + i] != 1

        @pl.when(passes)
        def _():
            passers[used] = i
            passers[used + 1] = i

        return used + passes.astype(jnp.int32)

    used = lax.fori_loop(0, SHARE, note, 0)

    def lanes(i):
        return pl.ds(pl.multiple_of(i * D, D), D)

    def pass_pair(t, carry):
        pair = [lanes(passers[2 * t]), lanes(passers[2 * t + 1])]
        row = lax.rem(lax.broadcasted_iota(jnp.int32, (2 * QB, QB), 0), QB)
        col = lax.broadcasted_iota(jnp.int32, (2 * QB, QB), 1)

        def scores(r):
            low, high = SINK + r, SINK + r + WIN + QB
            q_rows = jnp.concatenate([q[r : r + QB, place] for place in pair], 0)
            return dot(q_rows, jnp.concatenate([keys_t[:, :SINK], keys_t[:, low:high]], 1))

        ahead = scores(0)
        for r in range(0, rows, QB):
            s = ahead
            if r + QB < rows:
                ahead = scores(r + QB)
            low, high = SINK + r, SINK + r + WIN + QB
            s = jnp.concatenate(
                [
                    s[:, :SINK],
                    jnp.where(col > row, s[:, SINK : SINK + QB], -jnp.inf),
                    s[:, SINK + QB : SINK + WIN],
                    jnp.where(col <= row, s[:, SINK + WIN :], -jnp.inf),
                ],
                1,
            )
            top = jnp.max(s, axis=1, keepdims=True)
            p = jnp.exp2((s - top) * SCALE).astype(jnp.bfloat16)
            acc = dot(p, jnp.concatenate([vals[:SINK, :], vals[low:high, :]], 0))
            done = (acc[:, :D] / acc[:, D:]).astype(out.dtype)
            for n, place in enumerate(pair):
                out[r : r + QB, place] = done[n * QB : (n + 1) * QB]
        return carry

    lax.fori_loop(0, (used + 1) // 2, pass_pair, 0)

    def retrieve(i, slot):
        head = group * SHARE + i
        chosen = roles[head] == 1

        @pl.when(chosen)
        def _():
            row = lax.broadcasted_iota(jnp.int32, (BLK, NSL * BLK), 0)
            col = lax.broadcasted_iota(jnp.int32, (BLK, NSL * BLK), 1)
            causal = (col <= row) | (col >= BLK)
            lane = lax.broadcasted_iota(jnp.int32, (1, VB * BLK), 1)
            open_cols = lane < col_count[head] * BLK
            place = pl.ds(pl.multiple_of(slot * (VB * BLK), VB * BLK), VB * BLK)
            vert_v = jnp.concatenate(
                [far_v[place, :], jnp.ones((VB * BLK, D), jnp.bfloat16)], 1
            )
            q_head = q[:, lanes(i)]
            s_vert = jnp.where(open_cols, dot_nt(q_head, far_k[place, :]), -jnp.inf)
            p_verts, slashes = [], []

            def starts(r):
                return [
                    pl.multiple_of(WIN + r - diagonals[head, t] * BLK, BLK) for t in range(NSL)
                ]

            def scores(r):
                near_k = jnp.concatenate([keys[pl.ds(at, BLK), :] for at in starts(r)], 0)
                return dot_nt(q_head[r : r + BLK], near_k)

            nears = [scores(r) for r in range(0, rows, BLK)]
            for r in range(0, rows, BLK):
                near_v = jnp.concatenate(
                    [vals[pl.ds(SINK + at, BLK), :] for at in starts(r)], 0
                )
                s_near = jnp.where(causal, nears[r // BLK], -jnp.inf)
                s_far = s_vert[r : r + BLK]
                top = jnp.maximum(
                    jnp.max(s_near, axis=1, keepdims=True), jnp.max(s_far, axis=1, keepdims=True)
                )
                p_near = jnp.exp2((s_near - top) * SCALE).astype(jnp.bfloat16)
                p_verts.append(jnp.exp2((s_far - top) * SCALE).astype(jnp.bfloat16))
                slashes.append(dot(p_near, near_v))
            acc = dot(jnp.concatenate(p_verts, 0), vert_v) + jnp.concatenate(slashes, 0)
            out[:, lanes(i)] = (acc[:, :D] / acc[:, D:]).astype(out.dtype)

        return slot + chosen.astype(jnp.int32)

    lax.fori_loop(0, SHARE, retrieve, 0)


def attend(roles, col_count, diagonals, q, kv, previous, shared):
    rows, width = q.shape
    kv_count = kv.shape[1] // (2 * D)
    far_rows = MAX_RETRIEVERS * VB * BLK
    sink_block = 2 * kv_count * far_rows // SINK

    def whole(g, *_):
        return (0, g)

    def value(g, *_):
        return (0, kv_count + g)

    return pl.pallas_call(
        attend_kernel,
        grid_spec=pltpu.PrefetchScalarGridSpec(
            num_scalar_prefetch=3,
            grid=(kv_count,),
            in_specs=[
                pl.BlockSpec((rows, SHARE * D), whole),
                pl.BlockSpec((rows, D), whole),
                pl.BlockSpec((rows, D), value),
                pl.BlockSpec((WIN, D), whole),
                pl.BlockSpec((WIN, D), value),
                pl.BlockSpec((SINK, D), lambda g, *_: (sink_block + g, 0)),
                pl.BlockSpec((SINK, D), lambda g, *_: (sink_block + kv_count + g, 0)),
                pl.BlockSpec((far_rows, D), lambda g, *_: (g, 0)),
                pl.BlockSpec((far_rows, D), lambda g, *_: (kv_count + g, 0)),
            ],
            out_specs=pl.BlockSpec((rows, SHARE * D), whole),
            scratch_shapes=[
                pltpu.VMEM((D, SINK + WIN + rows), jnp.bfloat16),
                pltpu.VMEM((WIN + rows, D), jnp.bfloat16),
                pltpu.VMEM((SINK + WIN + rows, 2 * D), jnp.bfloat16),
                pltpu.SMEM((2 * SHARE,), jnp.int32),
            ],
        ),
        out_shape=jax.ShapeDtypeStruct((rows, width), jnp.bfloat16),
        compiler_params=pltpu.CompilerParams(vmem_limit_bytes=VMEM_LIMIT),
        cost_estimate=pl.CostEstimate(
            flops=8 * width * rows * (SINK + WIN + QB),
            bytes_accessed=4 * rows * width,
            transcendentals=width // D * rows * (SINK + WIN + QB),
        ),
        name="attend",
    )(roles, col_count, diagonals, q, kv, kv, previous, previous, shared, shared, shared, shared)


def shards(queries, keys, values, prefix_keys, prefix_values, roles, columns, col_count, diagonals):
    seq_size = lax.axis_size("seq")
    seq = lax.axis_index("seq").astype(jnp.int32).reshape(1)
    kv_count = prefix_keys.shape[1] // D
    needed = 2 * kv_count * (MAX_RETRIEVERS * VB * BLK + SINK)
    unit = 2 * 16 * seq_size
    rows = -(-needed // unit) * unit
    mine = collect(seq, roles, columns, col_count, prefix_keys, prefix_values, rows)
    shared, q, kv, previous = share(mine, queries, keys, values, prefix_keys, prefix_values)
    return attend(roles, col_count, diagonals, q, kv, previous, shared)


def solution(mesh):
    placed = (
        P(("seq", "head"), None),
        P(("seq", "head"), None),
        P(("seq", "head"), None),
        P("seq", "head"),
        P("seq", "head"),
        P("head"),
        P("head", None),
        P("head"),
        P("head", None),
    )
    return jax.shard_map(
        shards, mesh=mesh, in_specs=placed, out_specs=P("seq", "head"), check_vma=False
    )
```

```python
import functools
import math

import jax
import jax.numpy as jnp
from jax import lax
from jax.experimental import pallas as pl
from jax.experimental.pallas import tpu as pltpu
from jax.sharding import PartitionSpec as P

QUERY_HEADS = 64
KEY_VALUE_HEADS = 8
SHARE = QUERY_HEADS // KEY_VALUE_HEADS
D = 128
SINK = 128
WIN = 512
BLK = 64
VB = 6
NSL = 4
MAX_RETRIEVERS = 4
QB = 128
SCALE = math.log2(math.e) / math.sqrt(D)
VMEM_LIMIT = 40 * 1024 * 1024


def dot_nt(a, b):
    return lax.dot_general(a, b, (((1,), (1,)), ((), ())), preferred_element_type=jnp.float32)


def dot(a, b):
    return jnp.dot(a, b, preferred_element_type=jnp.float32)


def collect_kernel(seq, roles, columns, col_count, pk, pv, out, sem, sink_sem):
    blocks_dev = pk.shape[0] // BLK
    kv_count = pk.shape[1] // D
    slots = kv_count * MAX_RETRIEVERS
    out[...] = jnp.zeros_like(out)

    def copies(head, slot, c, col):
        local = col - seq[0] * blocks_dev
        rows = pl.ds(pl.multiple_of(local * BLK, BLK), BLK)
        cols = pl.ds(pl.multiple_of((head // SHARE) * D, D), D)
        t = slot * VB + c
        first = pl.ds(pl.multiple_of(t * BLK, BLK), BLK)
        second = pl.ds(pl.multiple_of((slots * VB + t) * BLK, BLK), BLK)
        return (
            pltpu.make_async_copy(pk.at[rows, cols], out.at[first, :], sem.at[0, t]),
            pltpu.make_async_copy(pv.at[rows, cols], out.at[second, :], sem.at[1, t]),
        )

    def sinks():
        base = 2 * slots * VB * BLK
        return [
            pltpu.make_async_copy(
                ref.at[pl.ds(0, SINK), pl.ds(g * D, D)],
                out.at[pl.ds(base + (part * kv_count + g) * SINK, SINK), :],
                sink_sem.at[part, g],
            )
            for part, ref in enumerate((pk, pv))
            for g in range(kv_count)
        ]

    def each(act):
        def visit(head, rank):
            rank = jnp.where(lax.rem(head, SHARE) == 0, 0, rank)
            chosen = roles[head] == 1

            @pl.when(chosen)
            def _():
                slot = (head // SHARE) * MAX_RETRIEVERS + rank
                for c in range(VB):
                    col = columns[head, c]

                    @pl.when((c < col_count[head]) & (col // blocks_dev == seq[0]))
                    def _():
                        for copy in copies(head, slot, c, col):
                            act(copy)

            return rank + chosen.astype(jnp.int32)

        lax.fori_loop(0, kv_count * SHARE, visit, 0)

        @pl.when(seq[0] == 0)
        def _():
            for copy in sinks():
                act(copy)

    each(lambda copy: copy.start())
    each(lambda copy: copy.wait())


def collect(seq, roles, columns, col_count, prefix_keys, prefix_values, rows):
    kv_count = prefix_keys.shape[1] // D
    return pl.pallas_call(
        collect_kernel,
        grid_spec=pltpu.PrefetchScalarGridSpec(
            num_scalar_prefetch=4,
            grid=(1,),
            in_specs=[pl.BlockSpec(memory_space=pltpu.HBM)] * 2,
            out_specs=pl.BlockSpec((rows, D), lambda i, *_: (0, 0)),
            scratch_shapes=[
                pltpu.SemaphoreType.DMA((2, kv_count * MAX_RETRIEVERS * VB)),
                pltpu.SemaphoreType.DMA((2, kv_count)),
            ],
        ),
        out_shape=jax.ShapeDtypeStruct((rows, D), jnp.bfloat16),
        compiler_params=pltpu.CompilerParams(vmem_limit_bytes=VMEM_LIMIT),
        name="collect_columns",
    )(seq, roles, columns, col_count, prefix_keys, prefix_values)


def share_kernel(
    size,
    heads,
    orders,
    mine,
    queries,
    keys,
    values,
    cache_k,
    cache_v,
    out,
    q_out,
    kv_out,
    previous,
    acc,
    landed,
    send_sem,
    recv_sem,
    swap_send,
    swap_recv,
    tail_send,
    tail_recv,
    own_sem,
):
    me = lax.axis_index("seq")
    my_head = lax.axis_index("head")
    right, left = lax.rem(me + 1, size), lax.rem(me + size - 1, size)
    bits = len(orders[0])
    barrier = pltpu.get_barrier_semaphore()

    def bit_of(b):
        return lax.rem(me // (1 << b), 2)

    def partner(b):
        return me + (1 - 2 * bit_of(b)) * (1 << b)

    for b in range(bits):
        pl.semaphore_signal(
            barrier, inc=1, device_id={"seq": partner(b)}, device_id_type=pl.DeviceIdType.MESH
        )
    for d in range(1, heads):
        pl.semaphore_signal(
            barrier,
            inc=1,
            device_id={"head": lax.rem(my_head + d, heads)},
            device_id_type=pl.DeviceIdType.MESH,
        )
    for neighbour in (left, right):
        pl.semaphore_signal(
            barrier, inc=1, device_id={"seq": neighbour}, device_id_type=pl.DeviceIdType.MESH
        )
    pl.semaphore_wait(barrier, bits + heads + 1)

    rows_in, cache_width = keys.shape[0], cache_k.shape[1]
    my_rows = pl.ds(pl.multiple_of(my_head * rows_in, 16), rows_in)
    swaps = (
        (keys, kv_out.at[my_rows, pl.ds(0, cache_width)], cache_width),
        (values, kv_out.at[my_rows, pl.ds(cache_width, cache_width)], cache_width),
        (queries, q_out.at[my_rows, :], q_out.shape[1]),
    )
    swapped = []
    for n, (source, target, width) in enumerate(swaps):
        row = []
        for d in range(heads):
            to = lax.rem(my_head + d, heads)
            block = source.at[:, pl.ds(pl.multiple_of(to * width, D), width)]
            if d == 0:
                copy = pltpu.make_async_copy(block, target, own_sem.at[n])
            else:
                copy = pltpu.make_async_remote_copy(
                    src_ref=block,
                    dst_ref=target,
                    send_sem=swap_send.at[n, d - 1],
                    recv_sem=swap_recv.at[n, d - 1],
                    device_id={"head": to},
                    device_id_type=pl.DeviceIdType.MESH,
                )
            copy.start()
            row.append(copy)
        swapped.append(row)

    def tails(cached):
        copies = []
        for n, cache in enumerate((cache_k, cache_v)):
            place = pl.ds(n * cache_width, cache_width)
            if cached:
                source = cache.at[pl.ds(cache.shape[0] - WIN, WIN), :]
            else:
                source = kv_out.at[pl.ds(kv_out.shape[0] - WIN, WIN), place]
            copies.append(
                pltpu.make_async_remote_copy(
                    src_ref=source,
                    dst_ref=previous.at[:, place],
                    send_sem=tail_send.at[n],
                    recv_sem=tail_recv.at[n],
                    device_id={"seq": right},
                    device_id_type=pl.DeviceIdType.MESH,
                )
            )
        return copies

    def pass_tails():
        for row in swapped[:2]:
            for copy in row:
                copy.wait()

        @pl.when(me == size - 1)
        def _():
            for copy in tails(True):
                copy.start()

        @pl.when(me != size - 1)
        def _():
            for copy in tails(False):
                copy.start()

    streams = len(orders)
    part = mine.shape[0] // streams
    low = [part * w for w in range(streams)]
    length = [part] * streams
    started = {}

    def at(start, n):
        return pl.ds(pl.multiple_of(start, 16), n)

    def move(src, dst, w, step, b):
        copy = pltpu.make_async_remote_copy(
            src_ref=src,
            dst_ref=dst,
            send_sem=send_sem.at[w, step],
            recv_sem=recv_sem.at[w, step],
            device_id={"seq": partner(b)},
            device_id_type=pl.DeviceIdType.MESH,
        )
        copy.start()
        started[w, step] = copy

    def halve(w, step):
        b = orders[w][step]
        half = length[w] // 2
        source = mine if step == 0 else acc
        other = low[w] + (1 - bit_of(b)) * half
        place = part * w + part - length[w]
        move(source.at[at(other, half), :], landed.at[pl.ds(place, half), :], w, step, b)

    def add(w, step):
        b = orders[w][step]
        half = length[w] // 2
        source = mine if step == 0 else acc
        place = part * w + part - length[w]
        keep = at(low[w] + bit_of(b) * half, half)
        started[w, step].wait()
        into = out if step == bits - 1 else acc
        into[keep, :] = source[keep, :] + landed[pl.ds(place, half), :]
        low[w] = low[w] + bit_of(b) * half
        length[w] = half

    def double(w, step):
        b = orders[w][2 * bits - 1 - step]
        whole = out.at[at(low[w], length[w]), :]
        move(whole, whole, w, step, b)

    def join(w, step):
        b = orders[w][2 * bits - 1 - step]
        started[w, step].wait()
        low[w] = low[w] - bit_of(b) * length[w]
        length[w] = 2 * length[w]

    for step in range(2 * bits + 1):
        for w in range(streams):
            if 0 < step <= bits:
                add(w, step - 1)
            elif step > bits:
                join(w, step - 1)
            if step < bits:
                halve(w, step)
            elif step < 2 * bits:
                double(w, step)
        if step == 1:
            pass_tails()
    for copy in tails(False):
        copy.wait()
    for copy in swapped[2]:
        copy.wait()


def share(mine, queries, keys, values, prefix_keys, prefix_values):
    size, heads = lax.axis_size("seq"), lax.axis_size("head")
    bits = size.bit_length() - 1
    orders = [list(range(bits)), [0, *range(2, bits), 1]]
    rows = mine.shape[0]
    kind = mine.dtype
    span = keys.shape[0] * heads
    cache_width = prefix_keys.shape[1]
    anywhere = pl.BlockSpec(memory_space=pltpu.HBM)
    local = pl.BlockSpec(memory_space=pltpu.VMEM)
    return pl.pallas_call(
        functools.partial(share_kernel, size, heads, orders),
        out_shape=(
            jax.ShapeDtypeStruct(mine.shape, kind),
            jax.ShapeDtypeStruct((span, queries.shape[1] // heads), kind),
            jax.ShapeDtypeStruct((span, 2 * cache_width), kind),
            jax.ShapeDtypeStruct((WIN, 2 * cache_width), kind),
        ),
        in_specs=[local] + [anywhere] * 5,
        out_specs=(local, anywhere, anywhere, anywhere),
        scratch_shapes=[
            pltpu.VMEM((rows, D), kind),
            pltpu.VMEM((rows, D), kind),
            pltpu.SemaphoreType.DMA((len(orders), 2 * bits)),
            pltpu.SemaphoreType.DMA((len(orders), 2 * bits)),
            pltpu.SemaphoreType.DMA((3, heads - 1)),
            pltpu.SemaphoreType.DMA((3, heads - 1)),
            pltpu.SemaphoreType.DMA((2,)),
            pltpu.SemaphoreType.DMA((2,)),
            pltpu.SemaphoreType.DMA((3,)),
        ],
        compiler_params=pltpu.CompilerParams(
            collective_id=0, has_side_effects=True, vmem_limit_bytes=VMEM_LIMIT
        ),
        cost_estimate=pl.CostEstimate(
            flops=10**10, bytes_accessed=8 * rows * D, transcendentals=0
        ),
        name="share_columns",
    )(mine, queries, keys, values, prefix_keys, prefix_values)


def attend_kernel(
    roles,
    col_count,
    diagonals,
    q,
    k,
    v,
    pk,
    pv,
    sk,
    sv,
    far_k,
    far_v,
    out,
    keys_t,
    keys,
    vals,
    passers,
):
    group = pl.program_id(0)
    rows = q.shape[0]

    keys_t[:, :SINK] = sk[...].T
    keys_t[:, SINK : SINK + WIN] = pk[...].T
    keys_t[:, SINK + WIN :] = k[...].T
    keys[:WIN, :] = pk[...]
    keys[WIN:, :] = k[...]
    vals[:SINK, :D] = sv[...]
    vals[SINK : SINK + WIN, :D] = pv[...]
    vals[SINK + WIN :, :D] = v[...]
    vals[:, D:] = jnp.ones_like(vals[:, D:])

    def note(i, used):
        passes = roles[group * SHARE + i] != 1

        @pl.when(passes)
        def _():
            passers[used] = i
            passers[used + 1] = i

        return used + passes.astype(jnp.int32)

    used = lax.fori_loop(0, SHARE, note, 0)

    def lanes(i):
        return pl.ds(pl.multiple_of(i * D, D), D)

    def pass_pair(t, carry):
        pair = [lanes(passers[2 * t]), lanes(passers[2 * t + 1])]
        row = lax.rem(lax.broadcasted_iota(jnp.int32, (2 * QB, QB), 0), QB)
        col = lax.broadcasted_iota(jnp.int32, (2 * QB, QB), 1)

        def scores(r):
            low, high = SINK + r, SINK + r + WIN + QB
            q_rows = jnp.concatenate([q[r : r + QB, place] for place in pair], 0)
            return dot(q_rows, jnp.concatenate([keys_t[:, :SINK], keys_t[:, low:high]], 1))

        ahead = scores(0)
        for r in range(0, rows, QB):
            s = ahead
            if r + QB < rows:
                ahead = scores(r + QB)
            low, high = SINK + r, SINK + r + WIN + QB
            s = jnp.concatenate(
                [
                    s[:, :SINK],
                    jnp.where(col > row, s[:, SINK : SINK + QB], -jnp.inf),
                    s[:, SINK + QB : SINK + WIN],
                    jnp.where(col <= row, s[:, SINK + WIN :], -jnp.inf),
                ],
                1,
            )
            top = jnp.max(s, axis=1, keepdims=True)
            p = jnp.exp2((s - top) * SCALE).astype(jnp.bfloat16)
            acc = dot(p, jnp.concatenate([vals[:SINK, :], vals[low:high, :]], 0))
            done = (acc[:, :D] / acc[:, D:]).astype(out.dtype)
            for n, place in enumerate(pair):
                out[r : r + QB, place] = done[n * QB : (n + 1) * QB]
        return carry

    lax.fori_loop(0, (used + 1) // 2, pass_pair, 0)

    def retrieve(i, slot):
        head = group * SHARE + i
        chosen = roles[head] == 1

        @pl.when(chosen)
        def _():
            row = lax.broadcasted_iota(jnp.int32, (BLK, NSL * BLK), 0)
            col = lax.broadcasted_iota(jnp.int32, (BLK, NSL * BLK), 1)
            causal = (col <= row) | (col >= BLK)
            lane = lax.broadcasted_iota(jnp.int32, (1, VB * BLK), 1)
            open_cols = lane < col_count[head] * BLK
            place = pl.ds(pl.multiple_of(slot * (VB * BLK), VB * BLK), VB * BLK)
            vert_v = jnp.concatenate(
                [far_v[place, :], jnp.ones((VB * BLK, D), jnp.bfloat16)], 1
            )
            q_head = q[:, lanes(i)]
            s_vert = jnp.where(open_cols, dot_nt(q_head, far_k[place, :]), -jnp.inf)
            p_verts, slashes = [], []

            def starts(r):
                return [
                    pl.multiple_of(WIN + r - diagonals[head, t] * BLK, BLK) for t in range(NSL)
                ]

            def scores(r):
                near_k = jnp.concatenate([keys[pl.ds(at, BLK), :] for at in starts(r)], 0)
                return dot_nt(q_head[r : r + BLK], near_k)

            nears = [scores(r) for r in range(0, rows, BLK)]
            for r in range(0, rows, BLK):
                near_v = jnp.concatenate(
                    [vals[pl.ds(SINK + at, BLK), :] for at in starts(r)], 0
                )
                s_near = jnp.where(causal, nears[r // BLK], -jnp.inf)
                s_far = s_vert[r : r + BLK]
                top = jnp.maximum(
                    jnp.max(s_near, axis=1, keepdims=True), jnp.max(s_far, axis=1, keepdims=True)
                )
                p_near = jnp.exp2((s_near - top) * SCALE).astype(jnp.bfloat16)
                p_verts.append(jnp.exp2((s_far - top) * SCALE).astype(jnp.bfloat16))
                slashes.append(dot(p_near, near_v))
            acc = dot(jnp.concatenate(p_verts, 0), vert_v) + jnp.concatenate(slashes, 0)
            out[:, lanes(i)] = (acc[:, :D] / acc[:, D:]).astype(out.dtype)

        return slot + chosen.astype(jnp.int32)

    lax.fori_loop(0, SHARE, retrieve, 0)


def attend(roles, col_count, diagonals, q, kv, previous, shared):
    rows, width = q.shape
    kv_count = kv.shape[1] // (2 * D)
    far_rows = MAX_RETRIEVERS * VB * BLK
    sink_block = 2 * kv_count * far_rows // SINK

    def whole(g, *_):
        return (0, g)

    def value(g, *_):
        return (0, kv_count + g)

    return pl.pallas_call(
        attend_kernel,
        grid_spec=pltpu.PrefetchScalarGridSpec(
            num_scalar_prefetch=3,
            grid=(kv_count,),
            in_specs=[
                pl.BlockSpec((rows, SHARE * D), whole),
                pl.BlockSpec((rows, D), whole),
                pl.BlockSpec((rows, D), value),
                pl.BlockSpec((WIN, D), whole),
                pl.BlockSpec((WIN, D), value),
                pl.BlockSpec((SINK, D), lambda g, *_: (sink_block + g, 0)),
                pl.BlockSpec((SINK, D), lambda g, *_: (sink_block + kv_count + g, 0)),
                pl.BlockSpec((far_rows, D), lambda g, *_: (g, 0)),
                pl.BlockSpec((far_rows, D), lambda g, *_: (kv_count + g, 0)),
            ],
            out_specs=pl.BlockSpec((rows, SHARE * D), whole),
            scratch_shapes=[
                pltpu.VMEM((D, SINK + WIN + rows), jnp.bfloat16),
                pltpu.VMEM((WIN + rows, D), jnp.bfloat16),
                pltpu.VMEM((SINK + WIN + rows, 2 * D), jnp.bfloat16),
                pltpu.SMEM((2 * SHARE,), jnp.int32),
            ],
        ),
        out_shape=jax.ShapeDtypeStruct((rows, width), jnp.bfloat16),
        compiler_params=pltpu.CompilerParams(vmem_limit_bytes=VMEM_LIMIT),
        cost_estimate=pl.CostEstimate(
            flops=8 * width * rows * (SINK + WIN + QB),
            bytes_accessed=4 * rows * width,
            transcendentals=width // D * rows * (SINK + WIN + QB),
        ),
        name="attend",
    )(roles, col_count, diagonals, q, kv, kv, previous, previous, shared, shared, shared, shared)


def shards(queries, keys, values, prefix_keys, prefix_values, roles, columns, col_count, diagonals):
    seq_size = lax.axis_size("seq")
    seq = lax.axis_index("seq").astype(jnp.int32).reshape(1)
    kv_count = prefix_keys.shape[1] // D
    needed = 2 * kv_count * (MAX_RETRIEVERS * VB * BLK + SINK)
    unit = 2 * 16 * seq_size
    rows = -(-needed // unit) * unit
    mine = collect(seq, roles, columns, col_count, prefix_keys, prefix_values, rows)
    shared, q, kv, previous = share(mine, queries, keys, values, prefix_keys, prefix_values)
    return attend(roles, col_count, diagonals, q, kv, previous, shared)


def solution(mesh):
    placed = (
        P(("seq", "head"), None),
        P(("seq", "head"), None),
        P(("seq", "head"), None),
        P("seq", "head"),
        P("seq", "head"),
        P("head"),
        P("head", None),
        P("head"),
        P("head", None),
    )
    return jax.shard_map(
        shards, mesh=mesh, in_specs=placed, out_specs=P("seq", "head"), check_vma=False
    )
```

```python
import functools
import math

import jax
import jax.numpy as jnp
from jax import lax
from jax.experimental import pallas as pl
from jax.experimental.pallas import tpu as pltpu
from jax.sharding import PartitionSpec as P

QUERY_HEADS = 64
KEY_VALUE_HEADS = 8
SHARE = QUERY_HEADS // KEY_VALUE_HEADS
D = 128
SINK = 128
WIN = 512
BLK = 64
VB = 6
NSL = 4
MAX_RETRIEVERS = 4
QB = 128
SCALE = math.log2(math.e) / math.sqrt(D)
VMEM_LIMIT = 40 * 1024 * 1024


def dot_nt(a, b):
    return lax.dot_general(a, b, (((1,), (1,)), ((), ())), preferred_element_type=jnp.float32)


def dot(a, b):
    return jnp.dot(a, b, preferred_element_type=jnp.float32)


def collect_kernel(seq, roles, columns, col_count, pk, pv, out, sem, sink_sem):
    blocks_dev = pk.shape[0] // BLK
    kv_count = pk.shape[1] // D
    slots = kv_count * MAX_RETRIEVERS
    out[...] = jnp.zeros_like(out)

    def copies(head, slot, c, col):
        local = col - seq[0] * blocks_dev
        rows = pl.ds(pl.multiple_of(local * BLK, BLK), BLK)
        cols = pl.ds(pl.multiple_of((head // SHARE) * D, D), D)
        t = slot * VB + c
        first = pl.ds(pl.multiple_of(t * BLK, BLK), BLK)
        second = pl.ds(pl.multiple_of((slots * VB + t) * BLK, BLK), BLK)
        return (
            pltpu.make_async_copy(pk.at[rows, cols], out.at[first, :], sem.at[0, t]),
            pltpu.make_async_copy(pv.at[rows, cols], out.at[second, :], sem.at[1, t]),
        )

    def sinks():
        base = 2 * slots * VB * BLK
        return [
            pltpu.make_async_copy(
                ref.at[pl.ds(0, SINK), pl.ds(g * D, D)],
                out.at[pl.ds(base + (part * kv_count + g) * SINK, SINK), :],
                sink_sem.at[part, g],
            )
            for part, ref in enumerate((pk, pv))
            for g in range(kv_count)
        ]

    def each(act):
        def visit(head, rank):
            rank = jnp.where(lax.rem(head, SHARE) == 0, 0, rank)
            chosen = roles[head] == 1

            @pl.when(chosen)
            def _():
                slot = (head // SHARE) * MAX_RETRIEVERS + rank
                for c in range(VB):
                    col = columns[head, c]

                    @pl.when((c < col_count[head]) & (col // blocks_dev == seq[0]))
                    def _():
                        for copy in copies(head, slot, c, col):
                            act(copy)

            return rank + chosen.astype(jnp.int32)

        lax.fori_loop(0, kv_count * SHARE, visit, 0)

        @pl.when(seq[0] == 0)
        def _():
            for copy in sinks():
                act(copy)

    each(lambda copy: copy.start())
    each(lambda copy: copy.wait())


def collect(seq, roles, columns, col_count, prefix_keys, prefix_values, rows):
    kv_count = prefix_keys.shape[1] // D
    return pl.pallas_call(
        collect_kernel,
        grid_spec=pltpu.PrefetchScalarGridSpec(
            num_scalar_prefetch=4,
            grid=(1,),
            in_specs=[pl.BlockSpec(memory_space=pltpu.HBM)] * 2,
            out_specs=pl.BlockSpec((rows, D), lambda i, *_: (0, 0)),
            scratch_shapes=[
                pltpu.SemaphoreType.DMA((2, kv_count * MAX_RETRIEVERS * VB)),
                pltpu.SemaphoreType.DMA((2, kv_count)),
            ],
        ),
        out_shape=jax.ShapeDtypeStruct((rows, D), jnp.bfloat16),
        compiler_params=pltpu.CompilerParams(vmem_limit_bytes=VMEM_LIMIT),
        name="collect_columns",
    )(seq, roles, columns, col_count, prefix_keys, prefix_values)


def share_kernel(
    size,
    heads,
    orders,
    mine,
    queries,
    keys,
    values,
    cache_k,
    cache_v,
    out,
    q_out,
    kv_out,
    previous,
    acc,
    landed,
    send_sem,
    recv_sem,
    swap_send,
    swap_recv,
    tail_send,
    tail_recv,
    own_sem,
):
    me = lax.axis_index("seq")
    my_head = lax.axis_index("head")
    right, left = lax.rem(me + 1, size), lax.rem(me + size - 1, size)
    bits = len(orders[0])
    barrier = pltpu.get_barrier_semaphore()

    def bit_of(b):
        return lax.rem(me // (1 << b), 2)

    def partner(b):
        return me + (1 - 2 * bit_of(b)) * (1 << b)

    for b in range(bits):
        pl.semaphore_signal(
            barrier, inc=1, device_id={"seq": partner(b)}, device_id_type=pl.DeviceIdType.MESH
        )
    for d in range(1, heads):
        pl.semaphore_signal(
            barrier,
            inc=1,
            device_id={"head": lax.rem(my_head + d, heads)},
            device_id_type=pl.DeviceIdType.MESH,
        )
    for neighbour in (left, right):
        pl.semaphore_signal(
            barrier, inc=1, device_id={"seq": neighbour}, device_id_type=pl.DeviceIdType.MESH
        )
    pl.semaphore_wait(barrier, bits + heads + 1)

    rows_in, cache_width = keys.shape[0], cache_k.shape[1]
    my_rows = pl.ds(pl.multiple_of(my_head * rows_in, 16), rows_in)
    swaps = (
        (keys, kv_out.at[my_rows, pl.ds(0, cache_width)], cache_width),
        (values, kv_out.at[my_rows, pl.ds(cache_width, cache_width)], cache_width),
        (queries, q_out.at[my_rows, :], q_out.shape[1]),
    )
    swapped = []
    for n, (source, target, width) in enumerate(swaps):
        row = []
        for d in range(heads):
            to = lax.rem(my_head + d, heads)
            block = source.at[:, pl.ds(pl.multiple_of(to * width, D), width)]
            if d == 0:
                copy = pltpu.make_async_copy(block, target, own_sem.at[n])
            else:
                copy = pltpu.make_async_remote_copy(
                    src_ref=block,
                    dst_ref=target,
                    send_sem=swap_send.at[n, d - 1],
                    recv_sem=swap_recv.at[n, d - 1],
                    device_id={"head": to},
                    device_id_type=pl.DeviceIdType.MESH,
                )
            copy.start()
            row.append(copy)
        swapped.append(row)

    def tails(cached):
        copies = []
        for n, cache in enumerate((cache_k, cache_v)):
            place = pl.ds(n * cache_width, cache_width)
            if cached:
                source = cache.at[pl.ds(cache.shape[0] - WIN, WIN), :]
            else:
                source = kv_out.at[pl.ds(kv_out.shape[0] - WIN, WIN), place]
            copies.append(
                pltpu.make_async_remote_copy(
                    src_ref=source,
                    dst_ref=previous.at[:, place],
                    send_sem=tail_send.at[n],
                    recv_sem=tail_recv.at[n],
                    device_id={"seq": right},
                    device_id_type=pl.DeviceIdType.MESH,
                )
            )
        return copies

    def pass_tails():
        for row in swapped[:2]:
            for copy in row:
                copy.wait()

        @pl.when(me == size - 1)
        def _():
            for copy in tails(True):
                copy.start()

        @pl.when(me != size - 1)
        def _():
            for copy in tails(False):
                copy.start()

    streams = len(orders)
    part = mine.shape[0] // streams
    low = [part * w for w in range(streams)]
    length = [part] * streams
    started = {}

    def at(start, n):
        return pl.ds(pl.multiple_of(start, 16), n)

    def move(src, dst, w, step, b):
        copy = pltpu.make_async_remote_copy(
            src_ref=src,
            dst_ref=dst,
            send_sem=send_sem.at[w, step],
            recv_sem=recv_sem.at[w, step],
            device_id={"seq": partner(b)},
            device_id_type=pl.DeviceIdType.MESH,
        )
        copy.start()
        started[w, step] = copy

    def halve(w, step):
        b = orders[w][step]
        half = length[w] // 2
        source = mine if step == 0 else acc
        other = low[w] + (1 - bit_of(b)) * half
        place = part * w + part - length[w]
        move(source.at[at(other, half), :], landed.at[pl.ds(place, half), :], w, step, b)

    def add(w, step):
        b = orders[w][step]
        half = length[w] // 2
        source = mine if step == 0 else acc
        place = part * w + part - length[w]
        keep = at(low[w] + bit_of(b) * half, half)
        started[w, step].wait()
        into = out if step == bits - 1 else acc
        into[keep, :] = source[keep, :] + landed[pl.ds(place, half), :]
        low[w] = low[w] + bit_of(b) * half
        length[w] = half

    def double(w, step):
        b = orders[w][2 * bits - 1 - step]
        whole = out.at[at(low[w], length[w]), :]
        move(whole, whole, w, step, b)

    def join(w, step):
        b = orders[w][2 * bits - 1 - step]
        started[w, step].wait()
        low[w] = low[w] - bit_of(b) * length[w]
        length[w] = 2 * length[w]

    for step in range(2 * bits + 1):
        for w in range(streams):
            if 0 < step <= bits:
                add(w, step - 1)
            elif step > bits:
                join(w, step - 1)
            if step < bits:
                halve(w, step)
            elif step < 2 * bits:
                double(w, step)
        if step == 1:
            pass_tails()
    for copy in tails(False):
        copy.wait()
    for copy in swapped[2]:
        copy.wait()


def share(mine, queries, keys, values, prefix_keys, prefix_values):
    size, heads = lax.axis_size("seq"), lax.axis_size("head")
    bits = size.bit_length() - 1
    orders = [list(range(bits)), [0, 2, 1, *range(3, bits)]]
    rows = mine.shape[0]
    kind = mine.dtype
    span = keys.shape[0] * heads
    cache_width = prefix_keys.shape[1]
    anywhere = pl.BlockSpec(memory_space=pltpu.HBM)
    local = pl.BlockSpec(memory_space=pltpu.VMEM)
    return pl.pallas_call(
        functools.partial(share_kernel, size, heads, orders),
        out_shape=(
            jax.ShapeDtypeStruct(mine.shape, kind),
            jax.ShapeDtypeStruct((span, queries.shape[1] // heads), kind),
            jax.ShapeDtypeStruct((span, 2 * cache_width), kind),
            jax.ShapeDtypeStruct((WIN, 2 * cache_width), kind),
        ),
        in_specs=[local] + [anywhere] * 5,
        out_specs=(local, anywhere, anywhere, anywhere),
        scratch_shapes=[
            pltpu.VMEM((rows, D), kind),
            pltpu.VMEM((rows, D), kind),
            pltpu.SemaphoreType.DMA((len(orders), 2 * bits)),
            pltpu.SemaphoreType.DMA((len(orders), 2 * bits)),
            pltpu.SemaphoreType.DMA((3, heads - 1)),
            pltpu.SemaphoreType.DMA((3, heads - 1)),
            pltpu.SemaphoreType.DMA((2,)),
            pltpu.SemaphoreType.DMA((2,)),
            pltpu.SemaphoreType.DMA((3,)),
        ],
        compiler_params=pltpu.CompilerParams(
            collective_id=0, has_side_effects=True, vmem_limit_bytes=VMEM_LIMIT
        ),
        cost_estimate=pl.CostEstimate(
            flops=10**10, bytes_accessed=8 * rows * D, transcendentals=0
        ),
        name="share_columns",
    )(mine, queries, keys, values, prefix_keys, prefix_values)


def attend_kernel(
    roles,
    col_count,
    diagonals,
    q,
    k,
    v,
    pk,
    pv,
    sk,
    sv,
    far_k,
    far_v,
    out,
    keys_t,
    keys,
    vals,
    passers,
):
    group = pl.program_id(0)
    rows = q.shape[0]

    keys_t[:, :SINK] = sk[...].T
    keys_t[:, SINK : SINK + WIN] = pk[...].T
    keys_t[:, SINK + WIN :] = k[...].T
    keys[:WIN, :] = pk[...]
    keys[WIN:, :] = k[...]
    vals[:SINK, :D] = sv[...]
    vals[SINK : SINK + WIN, :D] = pv[...]
    vals[SINK + WIN :, :D] = v[...]
    vals[:, D:] = jnp.ones_like(vals[:, D:])

    def note(i, used):
        passes = roles[group * SHARE + i] != 1

        @pl.when(passes)
        def _():
            passers[used] = i
            passers[used + 1] = i

        return used + passes.astype(jnp.int32)

    used = lax.fori_loop(0, SHARE, note, 0)

    def lanes(i):
        return pl.ds(pl.multiple_of(i * D, D), D)

    def pass_pair(t, carry):
        pair = [lanes(passers[2 * t]), lanes(passers[2 * t + 1])]
        row = lax.rem(lax.broadcasted_iota(jnp.int32, (2 * QB, QB), 0), QB)
        col = lax.broadcasted_iota(jnp.int32, (2 * QB, QB), 1)

        def scores(r):
            low, high = SINK + r, SINK + r + WIN + QB
            q_rows = jnp.concatenate([q[r : r + QB, place] for place in pair], 0)
            return dot(q_rows, jnp.concatenate([keys_t[:, :SINK], keys_t[:, low:high]], 1))

        ahead = scores(0)
        for r in range(0, rows, QB):
            s = ahead
            if r + QB < rows:
                ahead = scores(r + QB)
            low, high = SINK + r, SINK + r + WIN + QB
            s = jnp.concatenate(
                [
                    s[:, :SINK],
                    jnp.where(col > row, s[:, SINK : SINK + QB], -jnp.inf),
                    s[:, SINK + QB : SINK + WIN],
                    jnp.where(col <= row, s[:, SINK + WIN :], -jnp.inf),
                ],
                1,
            )
            top = jnp.max(s, axis=1, keepdims=True)
            p = jnp.exp2((s - top) * SCALE).astype(jnp.bfloat16)
            acc = dot(p, jnp.concatenate([vals[:SINK, :], vals[low:high, :]], 0))
            done = (acc[:, :D] / acc[:, D:]).astype(out.dtype)
            for n, place in enumerate(pair):
                out[r : r + QB, place] = done[n * QB : (n + 1) * QB]
        return carry

    lax.fori_loop(0, (used + 1) // 2, pass_pair, 0)

    def retrieve(i, slot):
        head = group * SHARE + i
        chosen = roles[head] == 1

        @pl.when(chosen)
        def _():
            row = lax.broadcasted_iota(jnp.int32, (BLK, NSL * BLK), 0)
            col = lax.broadcasted_iota(jnp.int32, (BLK, NSL * BLK), 1)
            causal = (col <= row) | (col >= BLK)
            lane = lax.broadcasted_iota(jnp.int32, (1, VB * BLK), 1)
            open_cols = lane < col_count[head] * BLK
            place = pl.ds(pl.multiple_of(slot * (VB * BLK), VB * BLK), VB * BLK)
            vert_v = jnp.concatenate(
                [far_v[place, :], jnp.ones((VB * BLK, D), jnp.bfloat16)], 1
            )
            q_head = q[:, lanes(i)]
            s_vert = jnp.where(open_cols, dot_nt(q_head, far_k[place, :]), -jnp.inf)
            p_verts, slashes = [], []

            def starts(r):
                return [
                    pl.multiple_of(WIN + r - diagonals[head, t] * BLK, BLK) for t in range(NSL)
                ]

            def scores(r):
                near_k = jnp.concatenate([keys[pl.ds(at, BLK), :] for at in starts(r)], 0)
                return dot_nt(q_head[r : r + BLK], near_k)

            nears = [scores(r) for r in range(0, rows, BLK)]
            for r in range(0, rows, BLK):
                near_v = jnp.concatenate(
                    [vals[pl.ds(SINK + at, BLK), :] for at in starts(r)], 0
                )
                s_near = jnp.where(causal, nears[r // BLK], -jnp.inf)
                s_far = s_vert[r : r + BLK]
                top = jnp.maximum(
                    jnp.max(s_near, axis=1, keepdims=True), jnp.max(s_far, axis=1, keepdims=True)
                )
                p_near = jnp.exp2((s_near - top) * SCALE).astype(jnp.bfloat16)
                p_verts.append(jnp.exp2((s_far - top) * SCALE).astype(jnp.bfloat16))
                slashes.append(dot(p_near, near_v))
            acc = dot(jnp.concatenate(p_verts, 0), vert_v) + jnp.concatenate(slashes, 0)
            out[:, lanes(i)] = (acc[:, :D] / acc[:, D:]).astype(out.dtype)

        return slot + chosen.astype(jnp.int32)

    lax.fori_loop(0, SHARE, retrieve, 0)


def attend(roles, col_count, diagonals, q, kv, previous, shared):
    rows, width = q.shape
    kv_count = kv.shape[1] // (2 * D)
    far_rows = MAX_RETRIEVERS * VB * BLK
    sink_block = 2 * kv_count * far_rows // SINK

    def whole(g, *_):
        return (0, g)

    def value(g, *_):
        return (0, kv_count + g)

    return pl.pallas_call(
        attend_kernel,
        grid_spec=pltpu.PrefetchScalarGridSpec(
            num_scalar_prefetch=3,
            grid=(kv_count,),
            in_specs=[
                pl.BlockSpec((rows, SHARE * D), whole),
                pl.BlockSpec((rows, D), whole),
                pl.BlockSpec((rows, D), value),
                pl.BlockSpec((WIN, D), whole),
                pl.BlockSpec((WIN, D), value),
                pl.BlockSpec((SINK, D), lambda g, *_: (sink_block + g, 0)),
                pl.BlockSpec((SINK, D), lambda g, *_: (sink_block + kv_count + g, 0)),
                pl.BlockSpec((far_rows, D), lambda g, *_: (g, 0)),
                pl.BlockSpec((far_rows, D), lambda g, *_: (kv_count + g, 0)),
            ],
            out_specs=pl.BlockSpec((rows, SHARE * D), whole),
            scratch_shapes=[
                pltpu.VMEM((D, SINK + WIN + rows), jnp.bfloat16),
                pltpu.VMEM((WIN + rows, D), jnp.bfloat16),
                pltpu.VMEM((SINK + WIN + rows, 2 * D), jnp.bfloat16),
                pltpu.SMEM((2 * SHARE,), jnp.int32),
            ],
        ),
        out_shape=jax.ShapeDtypeStruct((rows, width), jnp.bfloat16),
        compiler_params=pltpu.CompilerParams(vmem_limit_bytes=VMEM_LIMIT),
        cost_estimate=pl.CostEstimate(
            flops=8 * width * rows * (SINK + WIN + QB),
            bytes_accessed=4 * rows * width,
            transcendentals=width // D * rows * (SINK + WIN + QB),
        ),
        name="attend",
    )(roles, col_count, diagonals, q, kv, kv, previous, previous, shared, shared, shared, shared)


def shards(queries, keys, values, prefix_keys, prefix_values, roles, columns, col_count, diagonals):
    seq_size = lax.axis_size("seq")
    seq = lax.axis_index("seq").astype(jnp.int32).reshape(1)
    kv_count = prefix_keys.shape[1] // D
    needed = 2 * kv_count * (MAX_RETRIEVERS * VB * BLK + SINK)
    unit = 2 * 16 * seq_size
    rows = -(-needed // unit) * unit
    mine = collect(seq, roles, columns, col_count, prefix_keys, prefix_values, rows)
    shared, q, kv, previous = share(mine, queries, keys, values, prefix_keys, prefix_values)
    return attend(roles, col_count, diagonals, q, kv, previous, shared)


def solution(mesh):
    placed = (
        P(("seq", "head"), None),
        P(("seq", "head"), None),
        P(("seq", "head"), None),
        P("seq", "head"),
        P("seq", "head"),
        P("head"),
        P("head", None),
        P("head"),
        P("head", None),
    )
    return jax.shard_map(
        shards, mesh=mesh, in_specs=placed, out_specs=P("seq", "head"), check_vma=False
    )
```
